512 devices in a mesh: dp: 4 (over x), expert: 128 (over y, z, core).
Axes of the slice: x: 4, y: 8, z: 8, core: 2. Of those that a mesh axis runs over, the one named last changes fastest.
Arguments:
- tokens: bfloat16 [512, 128, 1280], P(('dp', 'expert')), may hold values from -16 to 16
- ln_gain: bfloat16 [1280], replicated, may hold values from 0.25 to 1.75
- w_router: bfloat16 [1280, 128], replicated, may hold values from -0.3354102 to 0.3354102
- w_in: bfloat16 [128, 1280, 2560], P('expert', None, 'dp'), may hold values from -0.15625 to 0.15625
- w_out: bfloat16 [128, 2560, 1280], P('expert', 'dp'), may hold values from -0.125 to 0.125
- expert_ids: int32 [512, 128], P(('dp', 'expert')), may hold values from 0 to 127
- keep: int32 [512, 128], P(('dp', 'expert')), may hold values from 0 to 1, as said below
- slots: int32 [512, 128], P(('dp', 'expert')), may hold values from 0 to 1, as said below
- logit_scale: float32 [1], replicated, may hold values from 10 to 400
Outputs:
- pair_loss: float32 [512], P(('dp', 'expert'))
- tokens_grad: bfloat16 [512, 128, 1280], P(('dp', 'expert'))
The draws below stay inside these ranges and needn't reach their ends.
Inputs may be any that keep to these rules, and one draw needn't show every extreme that they name: `keep`: among the 128 tokens of one group, at most 2 kept tokens name any one expert; in every draw some expert receives exactly 2 kept tokens from every group. Kept tokens of one group that name one expert have distinct slots; a dropped token's slot carries no meaning.
All inputs are finite; a program needn't handle non-finite values.
Results may differ from the reference program's by a relative error of at most 0.015.
Values may be sent and summed in bfloat16 or wider, within the bound.
A program may use at most 128 MiB of HBM per device.

```python
import math
import jax
import jax.numpy as jnp
from jax import lax

D = 1280
FF = 2560
SEQ = 64
PAIRS_DEV = 1
TOK_DEV = 128
EXPERTS = 128
CAP = 2
PAIRS = 512
N_DP = 4


def routing(key):
    blocks = PAIRS // PAIRS_DEV
    k_perm, k_one, k_two, k_prio, k_hot = jax.random.split(key, 5)
    expert_order = jax.random.permutation(k_perm, EXPERTS)
    first_draw = jax.random.randint(k_one, (blocks, TOK_DEV), 0, EXPERTS)
    second = jax.random.randint(k_two, (blocks, TOK_DEV), 0, EXPERTS)
    expert_pick = expert_order[jnp.minimum(first_draw, second)]
    priority = jax.vmap(lambda one_key: jax.random.permutation(one_key, TOK_DEV))(jax.random.split(k_prio, blocks))
    hot_expert = jax.random.randint(k_hot, (), 0, EXPERTS)
    expert_pick = jnp.where(priority < CAP, hot_expert, expert_pick).astype(jnp.int32)
    same_expert = expert_pick[:, :, None] == expert_pick[:, None, :]
    earlier = priority[:, None, :] < priority[:, :, None]
    rank_within = jnp.sum((same_expert & earlier).astype(jnp.int32), 2)
    kept_mask = (rank_within < CAP).astype(jnp.int32)
    slot_index = (rank_within % CAP).astype(jnp.int32)
    shape_out = (PAIRS, 2 * SEQ)
    return (expert_pick.reshape(shape_out), kept_mask.reshape(shape_out), slot_index.reshape(shape_out))


def router_weights(key):
    router_key = jax.random.fold_in(key, 101)
    values = jnp.clip(jax.random.normal(router_key, (D, EXPERTS), jnp.float32), -6.0, 6.0)
    return values * (2.0 / math.sqrt(D))


def draw_expert_ids(key, part):
    return routing(key)[0]


def draw_keep(key, part):
    return routing(key)[1]


def draw_slots(key, part):
    return routing(key)[2]


def draw_w_router(key, part):
    return router_weights(key).astype(jnp.bfloat16)


def draw_tokens(key, part):
    picked = routing(key)[0]
    router = router_weights(key)
    key = jax.random.fold_in(key, 11)
    k_topic = jax.random.fold_in(key, 0)
    k_pick = jax.random.fold_in(key, 1)
    k_mix = jax.random.fold_in(key, 2)
    k_noise = jax.random.fold_in(key, 3)
    k_lean = jax.random.fold_in(key, 5)
    topic_count = max(2, PAIRS // 8)
    topics = jax.random.normal(k_topic, (topic_count, D), jnp.float32)
    topic_pick = jax.random.randint(k_pick, (PAIRS, 2), 0, topic_count)
    centers = topics[topic_pick][:, :, None, :]
    noise_part = jax.random.normal(k_noise, (PAIRS, 2, SEQ, D), jnp.float32)
    columns = jnp.transpose(router)[picked.reshape(PAIRS * 2 * SEQ)] * (math.sqrt(D) / 2.0)
    lean = jax.random.uniform(k_lean, (PAIRS * 2 * SEQ, 1), jnp.float32, 0.6, 1.4) * (3.5 / math.sqrt(D))
    toward = (columns * lean).reshape(PAIRS, 2, SEQ, D)
    mix_share = jax.random.uniform(k_mix, (PAIRS, 2, 1, 1), jnp.float32, 0.55, 0.85)
    values = mix_share * centers + jnp.sqrt(1.0 - mix_share * mix_share) * noise_part + toward
    return jnp.clip(values, -16.0, 16.0).reshape(PAIRS, 2 * SEQ, D).astype(jnp.bfloat16)


def draw_logit_scale(key, part):
    key = jax.random.fold_in(key, 23)
    values = jnp.exp(jax.random.uniform(key, (1,), jnp.float32, math.log(10.0), math.log(30.0)))
    return values


def shard_levels(own_key, dims, cuts, least, top_value):
    level, own = 1.0, jax.random.fold_in(own_key, 6)
    for dim, parts in cuts:
        draws = jnp.exp(jax.random.uniform(jax.random.fold_in(own, dim), (parts,), jnp.float32, least / len(cuts), top_value / len(cuts)))
        level = level * jnp.repeat(draws, dims[dim] // parts).reshape([-1 if axis == dim else 1 for axis in range(len(dims))])
    return level


def gaussian(own_key, extent, scale, most, pieces=(), kind=jnp.bfloat16):
    entries = jax.random.normal(own_key, extent, jnp.float32) * scale
    if len(pieces) > 0:
        entries = shard_levels(own_key, extent, pieces, -0.22, 0.18) * entries
    return jnp.clip(entries, min=-most, max=most).astype(kind)


def setup_inputs(seed: int = 0) -> dict:
    key_of = jax.random.split(jax.random.key(seed), 10)
    tokens = draw_tokens(jax.random.fold_in(key_of[9], 71), 0)
    ln_gain = jnp.clip(1.0 + 0.15 * jax.random.normal(key_of[1], (D,), jnp.float32), 0.25, 1.75).astype(jnp.bfloat16)
    w_router = draw_w_router(jax.random.fold_in(key_of[9], 71), 0)
    w_in = gaussian(key_of[3], (EXPERTS, D, FF), D ** -0.5, 0.15625, ((0, 128), (2, 4)))
    w_out = gaussian(key_of[4], (EXPERTS, FF, D), FF ** -0.5, 0.125, ((0, 128), (1, 4)))
    expert_ids = draw_expert_ids(jax.random.fold_in(key_of[9], 71), 0)
    keep = draw_keep(jax.random.fold_in(key_of[9], 71), 0)
    slots = draw_slots(jax.random.fold_in(key_of[9], 71), 0)
    logit_scale = draw_logit_scale(jax.random.fold_in(key_of[9], 71), 0)
    return {"tokens": tokens, "ln_gain": ln_gain, "w_router": w_router, "w_in": w_in, "w_out": w_out, "expert_ids": expert_ids, "keep": keep, "slots": slots, "logit_scale": logit_scale}


norm_eps = 1e-06

def activation(values):
    return jax.nn.gelu(values, approximate=False)

def layer_norm(matrix_rows, ln_gain):
    centered = matrix_rows - lax.optimization_barrier(jnp.mean(matrix_rows, -1, keepdims=True))
    variance = lax.optimization_barrier(jnp.mean(centered * centered, -1, keepdims=True))
    return centered * lax.rsqrt(variance + norm_eps) * ln_gain.astype(jnp.float32)

def unit_rows(pooled):
    return pooled * lax.rsqrt(lax.optimization_barrier(jnp.sum(pooled * pooled, -1, keepdims=True)) + norm_eps)

def rounded_sum(block_parts):
    held_parts = lax.optimization_barrier(block_parts.astype(jnp.bfloat16))
    return lax.optimization_barrier(jnp.sum(held_parts.astype(jnp.float32), 0)).astype(jnp.bfloat16)

def expert_forward(matrix_rows, weight_in, weight_out):
    block_width = FF // N_DP
    pre_act = jnp.dot(matrix_rows, weight_in, preferred_element_type=jnp.float32)
    hidden_act = activation(pre_act).astype(jnp.bfloat16)
    block_parts = jnp.einsum('rkf,kfd->krd', hidden_act.reshape(matrix_rows.shape[0], N_DP, block_width).astype(jnp.float32), weight_out.reshape(N_DP, block_width, D).astype(jnp.float32))
    return rounded_sum(block_parts)

def expert_backward(matrix_rows, grad_rows, weight_in, weight_out):
    block_width = FF // N_DP
    pre_act = jnp.dot(matrix_rows, weight_in, preferred_element_type=jnp.float32)
    d_act = jnp.dot(grad_rows, weight_out.T, preferred_element_type=jnp.float32)
    _, pull_back = jax.vjp(activation, pre_act)
    d_pre = pull_back(d_act)[0].astype(jnp.bfloat16)
    block_parts = jnp.einsum('rkf,dkf->krd', d_pre.reshape(matrix_rows.shape[0], N_DP, block_width).astype(jnp.float32), weight_in.reshape(D, N_DP, block_width).astype(jnp.float32))
    return rounded_sum(block_parts)

def dispatch(matrix_rows, target, keep_f, blocks):
    group_index = jnp.broadcast_to(jnp.arange(blocks, dtype=jnp.int32)[:, None], target.shape)
    filled = jnp.zeros((blocks, EXPERTS * CAP, D), jnp.float32)
    filled = filled.at[group_index, target].add(matrix_rows.astype(jnp.float32) * keep_f[:, :, None])
    filled = filled.astype(jnp.bfloat16).reshape(blocks, EXPERTS, CAP, D)
    return jnp.swapaxes(filled, 0, 1).reshape(EXPERTS, blocks * CAP, D)

def collect(expert_rows, target, keep_f, blocks):
    back_rows = jnp.swapaxes(expert_rows.reshape(EXPERTS, blocks, CAP, D), 0, 1).reshape(blocks, EXPERTS * CAP, D)
    chosen = jnp.take_along_axis(back_rows, target[:, :, None], axis=1)
    return chosen.astype(jnp.float32) * keep_f[:, :, None]

def reference(tokens, ln_gain, w_router, w_in, w_out, expert_ids, keep, slots, logit_scale):
    blocks = PAIRS // PAIRS_DEV
    score_scale = logit_scale[0]
    rows_in = tokens.reshape(blocks, TOK_DEV, D).astype(jnp.float32)
    normed, norm_pull = jax.vjp(lambda values: layer_norm(values, ln_gain), rows_in)
    normed_b = normed.astype(jnp.bfloat16)
    routed = expert_ids.reshape(blocks, TOK_DEV)
    keep_f = keep.reshape(blocks, TOK_DEV).astype(jnp.float32)
    target = (routed * CAP + slots.reshape(blocks, TOK_DEV)).astype(jnp.int32)
    choose = (lax.broadcasted_iota(jnp.int32, (blocks, TOK_DEV, EXPERTS), 2) == routed[:, :, None]).astype(jnp.float32)
    logits = jnp.dot(normed_b.reshape(blocks * TOK_DEV, D), w_router, preferred_element_type=jnp.float32).reshape(blocks, TOK_DEV, EXPERTS)
    expo = jnp.exp(logits)
    probs = expo / lax.optimization_barrier(jnp.sum(expo, 2, keepdims=True))
    gate_val = lax.optimization_barrier(jnp.sum(probs * choose, 2))
    sent_rows = dispatch(normed_b, target, keep_f, blocks)
    expert_out = lax.map(lambda operands: expert_forward(operands[0], operands[1], operands[2]), (sent_rows, w_in, w_out))
    moe_rows = collect(expert_out, target, keep_f, blocks)
    mixed_rows = rows_in + (keep_f * gate_val)[:, :, None] * moe_rows
    pooled = lax.optimization_barrier(jnp.mean(mixed_rows.reshape(PAIRS, 2, SEQ, D), 2))
    unit_emb, unit_pull = jax.vjp(unit_rows, pooled)
    unit_b = unit_emb.astype(jnp.bfloat16)
    images = unit_b[:, 0]
    texts = unit_b[:, 1]
    scores = score_scale * jnp.dot(images, texts.T, preferred_element_type=jnp.float32)
    row_tot = jax.nn.logsumexp(scores, 1)
    col_tot = jax.nn.logsumexp(scores, 0)
    pair_loss = (row_tot + col_tot - 2.0 * jnp.diagonal(scores)) * 0.5
    weights = ((jnp.exp(scores - row_tot[:, None]) + jnp.exp(scores - col_tot[None, :])) * 0.5 - jnp.eye(PAIRS, dtype=jnp.float32)).astype(jnp.bfloat16)
    d_images = score_scale * jnp.dot(weights, texts, preferred_element_type=jnp.float32)
    d_texts = score_scale * jnp.dot(weights.T, images, preferred_element_type=jnp.float32)
    d_pooled = unit_pull(jnp.stack([d_images, d_texts], 1))[0]
    d_mixed = jnp.broadcast_to(d_pooled[:, :, None, :] / SEQ, (PAIRS, 2, SEQ, D)).reshape(blocks, TOK_DEV, D)
    d_moe = ((keep_f * gate_val)[:, :, None] * d_mixed).astype(jnp.bfloat16)
    grad_rows = dispatch(d_moe, target, keep_f, blocks)
    d_back = lax.map(lambda operands: expert_backward(operands[0], operands[1], operands[2], operands[3]), (sent_rows, grad_rows, w_in, w_out))
    d_normed_moe = collect(d_back, target, keep_f, blocks)
    d_gate = keep_f * lax.optimization_barrier(jnp.sum(d_mixed * moe_rows, 2)) * gate_val
    d_logit = d_gate[:, :, None] * (choose - probs)
    router_part = jnp.dot(d_logit.reshape(blocks * TOK_DEV, EXPERTS), w_router.astype(jnp.float32).T, precision=lax.Precision.HIGHEST).reshape(blocks, TOK_DEV, D)
    d_normed = d_normed_moe + router_part
    d_tokens = d_mixed + norm_pull(d_normed)[0]
    tokens_grad = (d_tokens * (128.0 * SEQ / score_scale)).astype(jnp.bfloat16).reshape(PAIRS, 2 * SEQ, D)
    return (pair_loss, tokens_grad)
```

```python
import functools

import jax
import jax.numpy as jnp
from jax import lax
from jax.experimental import pallas as pl
from jax.experimental.pallas import tpu as pltpu
from jax.sharding import PartitionSpec as P

MESH = pl.DeviceIdType.MESH
norm_eps = 1e-06
CHUNKS = 5
CORES = 2
SLOTS = 2


def activation(values):
    return 0.5 * values * (1.0 + lax.erf(values * (0.5**0.5)))


def activation_slope(values):
    bell = jnp.exp(-0.5 * values * values) * 0.3989422804014327
    return 0.5 * (1.0 + lax.erf(values * (0.5**0.5))) + values * bell


def layer_norm(matrix_rows, ln_gain):
    centered = matrix_rows - jnp.mean(matrix_rows, -1, keepdims=True)
    variance = jnp.mean(centered * centered, -1, keepdims=True)
    return centered * lax.rsqrt(variance + norm_eps) * ln_gain.astype(jnp.float32)


def unit_rows(pooled):
    return pooled * lax.rsqrt(jnp.sum(pooled * pooled, -1, keepdims=True) + norm_eps)


def chip_sides(experts):
    chips = experts // CORES
    side = 1
    while side * side < chips:
        side *= 2
    return side, chips // side


def near_first(count):
    offsets = []
    for step in range(1, count // 2 + 1):
        offsets.append(step)
        if count - step != step:
            offsets.append(count - step)
    return offsets


def send(src, dst, send_sem, recv_sem, device):
    pltpu.make_async_remote_copy(
        src_ref=src,
        dst_ref=dst,
        send_sem=send_sem,
        recv_sem=recv_sem,
        device_id=device,
        device_id_type=MESH,
    ).start()


def drain(ref, sem):
    pltpu.make_async_copy(ref, ref, sem).wait()


def greet(peers):
    barrier = pltpu.get_barrier_semaphore()
    for peer in peers:
        pl.semaphore_signal(barrier, inc=1, device_id=peer, device_id_type=MESH)
    pl.semaphore_wait(barrier, len(peers))


def from_slots(slot_table, matrix_rows):
    return jnp.einsum("st,sd->td", slot_table, matrix_rows, preferred_element_type=jnp.float32)


def moe_kernel(backward, ny, nz, *refs):
    if backward:
        src, w_in, w_out, pre, out = refs[:5]
        acc, slope = refs[-2:]
    else:
        src, w_in, w_out, out, pre = refs[:5]
        acc = pre
    ybuf, zsend, zbuf, xl, xr, xo, so, sr, sl, fl, fr, zs, zr, ys, yr = refs[5:20]
    ol, orr, keep_r, keep_l, own, hid, perm = refs[20:27]
    s_y, r_y, s_z, r_z, s_x, r_x, s_o, r_o = refs[27:35]
    s_p, r_p, s_q, r_q, s_zr, r_zr, s_yr, r_yr = refs[35:43]
    n, rows, width = ybuf.shape
    half = rows // 2
    top, low = pl.ds(0, half), pl.ds(half, half)
    nzc = nz * CORES
    yb, zb = nzc * SLOTS, ny * SLOTS
    dpn = lax.axis_size("dp")
    x = lax.axis_index("dp")
    rank = lax.axis_index("expert")
    y, zc = lax.div(rank, nzc), lax.rem(rank, nzc)
    right, left = (lax.rem(x + 1, dpn), rank), (lax.rem(x + dpn - 1, dpn), rank)

    def y_block(index):
        return pl.ds(pl.multiple_of(index * yb, yb), yb)

    def z_block(index):
        return pl.ds(pl.multiple_of(index * zb, zb), zb)

    y_peers = [lax.rem(y + k, ny) for k in near_first(ny)]
    z_peers = [lax.rem(zc + k, nzc) for k in near_first(nzc)]

    greet(
        [(x, peer * nzc + zc) for peer in y_peers]
        + [(x, y * nzc + peer) for peer in z_peers]
        + [right, left]
    )

    for t in range(n):
        for peer in y_peers:
            send(
                src.at[y_block(peer), pl.ds(t * width, width)],
                ybuf.at[t, y_block(y)],
                s_y.at[t],
                r_y.at[t],
                (x, peer * nzc + zc),
            )

    place = lax.broadcasted_iota(jnp.int32, (rows, rows), 0)
    col = lax.broadcasted_iota(jnp.int32, (rows, rows), 1)
    for k, (fine, coarse) in enumerate(((zb, yb), (yb, zb))):
        within = place & (fine - 1)
        want = (within >> 1) * coarse + (place >> (fine.bit_length() - 1)) * SLOTS + (within & 1)
        perm[k] = (col == want).astype(jnp.float32).astype(jnp.bfloat16)

    slab = 16

    def by_slab(step):
        def body(i, carry):
            at = pl.ds(pl.multiple_of(i * slab, slab), slab)
            for b in range(4):
                step(b, at)
            return carry

        lax.fori_loop(0, rows // slab, body, 0)

    if backward:

        def slope_step(b, at):
            slope[b, at, :] = activation_slope(pre[b, at, :])

        by_slab(slope_step)

    def cols(t):
        return slice(t * width, (t + 1) * width)

    def product_in(block, t):
        if backward:
            return lax.dot_general(
                block, w_out[:, cols(t)], (((1,), (1,)), ((), ())), preferred_element_type=jnp.float32
            )
        return jnp.dot(block, w_in[cols(t), :], preferred_element_type=jnp.float32)

    def product_out(b, t):
        if backward:
            return lax.dot_general(
                hid[b], w_in[cols(t), :], (((1,), (1,)), ((), ())), preferred_element_type=jnp.float32
            )
        return jnp.dot(hid[b], w_out[:, cols(t)], preferred_element_type=jnp.float32)

    def stage_z(t):
        ybuf[t, y_block(y), :] = src[y_block(y), cols(t)]
        drain(ybuf.at[t, pl.ds(0, rows - yb)], r_y.at[t])
        zsend[t] = jnp.dot(perm[0], ybuf[t], preferred_element_type=jnp.float32).astype(jnp.bfloat16)
        for peer in z_peers:
            send(
                zsend.at[t, z_block(peer)],
                zbuf.at[t, z_block(zc)],
                s_z.at[t],
                r_z.at[t],
                (x, y * nzc + peer),
            )
        zbuf[t, z_block(zc), :] = zsend[t, z_block(zc), :]

    def stage_x(t):
        drain(zbuf.at[t, pl.ds(0, rows - zb)], r_z.at[t])
        send(zbuf.at[t], xl.at[t], s_x.at[t, 0], r_x.at[t, 0], right)
        send(zbuf.at[t], xr.at[t], s_x.at[t, 1], r_x.at[t, 1], left)

    def stage_forward(t):
        drain(xl.at[t], r_x.at[t, 0])
        send(xl.at[t, top], xo.at[t, top], s_o.at[t, 0], r_o.at[t, 0], right)
        drain(xr.at[t], r_x.at[t, 1])
        send(xr.at[t, low], xo.at[t, low], s_o.at[t, 1], r_o.at[t, 1], left)

    def stage_in(t):
        drain(xo.at[t, top], r_o.at[t, 0])
        drain(xo.at[t, low], r_o.at[t, 1])
        for b, block in enumerate((zbuf, xl, xr, xo)):
            part = product_in(block[t], t)
            acc[b] = part if t == 0 else acc[b] + part

    for t in range(n + 3):
        if t < n:
            stage_z(t)
        if 0 <= t - 1 < n:
            stage_x(t - 1)
        if 0 <= t - 2 < n:
            stage_forward(t - 2)
        if 0 <= t - 3 < n:
            stage_in(t - 3)

    def hidden_step(b, at):
        values = acc[b, at, :]
        values = values * slope[b, at, :] if backward else activation(values)
        hid[b, at, :] = values.astype(jnp.bfloat16)

    by_slab(hidden_step)

    def stage_out(t):
        so[t] = product_out(3, t).astype(jnp.bfloat16)
        send(so.at[t, top], ol.at[t], s_p.at[t, 0], r_p.at[t, 0], right)
        send(so.at[t, low], orr.at[t], s_p.at[t, 1], r_p.at[t, 1], left)
        part = product_out(2, t)
        sr[t, half:, :] = part[half:].astype(jnp.bfloat16)
        send(sr.at[t, low], fl.at[t, low], s_q.at[t, 0], r_q.at[t, 0], right)
        keep_r[t] = part[:half]
        part = product_out(1, t)
        sl[t, :half, :] = part[:half].astype(jnp.bfloat16)
        send(sl.at[t, top], fr.at[t, top], s_q.at[t, 1], r_q.at[t, 1], left)
        keep_l[t] = part[half:]
        own[t] = product_out(0, t)

    def stage_add(t):
        drain(ol.at[t], r_p.at[t, 0])
        sr[t, :half, :] = (keep_r[t] + ol[t].astype(jnp.float32)).astype(jnp.bfloat16)
        send(sr.at[t, top], fl.at[t, top], s_q.at[t, 0], r_q.at[t, 0], right)
        drain(orr.at[t], r_p.at[t, 1])
        sl[t, half:, :] = (keep_l[t] + orr[t].astype(jnp.float32)).astype(jnp.bfloat16)
        send(sl.at[t, low], fr.at[t, low], s_q.at[t, 1], r_q.at[t, 1], left)

    def stage_back_z(t):
        drain(fl.at[t], r_q.at[t, 0])
        drain(fr.at[t], r_q.at[t, 1])
        total = own[t] + fl[t].astype(jnp.float32) + fr[t].astype(jnp.float32)
        zs[t] = total.astype(jnp.bfloat16)
        for peer in z_peers:
            send(
                zs.at[t, z_block(peer)],
                zr.at[t, z_block(zc)],
                s_zr.at[t],
                r_zr.at[t],
                (x, y * nzc + peer),
            )
        zr[t, z_block(zc), :] = zs[t, z_block(zc), :]

    def stage_back_y(t):
        drain(zr.at[t, pl.ds(0, rows - zb)], r_zr.at[t])
        ys[t] = jnp.dot(perm[1], zr[t], preferred_element_type=jnp.float32).astype(jnp.bfloat16)
        for peer in y_peers:
            send(
                ys.at[t, y_block(peer)],
                yr.at[t, y_block(y)],
                s_yr.at[t],
                r_yr.at[t],
                (x, peer * nzc + zc),
            )
        yr[t, y_block(y), :] = ys[t, y_block(y), :]

    def stage_store(t):
        drain(yr.at[t, pl.ds(0, rows - yb)], r_yr.at[t])
        out[:, cols(t)] = yr[t]

    for t in range(n + 4):
        if t < n:
            stage_out(t)
        if 0 <= t - 1 < n:
            stage_add(t - 1)
        if 0 <= t - 2 < n:
            stage_back_z(t - 2)
        if 0 <= t - 3 < n:
            stage_back_y(t - 3)
        if 0 <= t - 4 < n:
            stage_store(t - 4)

    for t in range(n):
        drain(ybuf.at[t, pl.ds(0, rows - yb)], s_y.at[t])
        drain(zsend.at[t, pl.ds(0, rows - zb)], s_z.at[t])
        drain(zs.at[t, pl.ds(0, rows - zb)], s_zr.at[t])
        drain(ys.at[t, pl.ds(0, rows - yb)], s_yr.at[t])
        for way in range(2):
            drain(zbuf.at[t], s_x.at[t, way])
            drain(xo.at[t, top], s_o.at[t, way])
            drain(so.at[t, top], s_p.at[t, way])
            drain(sr.at[t], s_q.at[t, way])


def moe_call(backward, experts, packed, w_in, w_out, pre=None):
    ny, nz = chip_sides(experts)
    rows, model_width = packed.shape
    hidden = w_in.shape[1]
    n, width = CHUNKS, model_width // CHUNKS
    half = rows // 2
    bf16, f32 = jnp.bfloat16, jnp.float32
    vmem = pl.BlockSpec(memory_space=pltpu.VMEM)
    dma = pltpu.SemaphoreType.DMA
    scratch = [pltpu.VMEM((n, rows, width), bf16) for _ in range(15)]
    scratch += [pltpu.VMEM((n, half, width), bf16) for _ in range(2)]
    scratch += [pltpu.VMEM((n, half, width), f32) for _ in range(2)]
    scratch += [pltpu.VMEM((n, rows, width), f32)]
    scratch += [pltpu.VMEM((4, rows, hidden), bf16), pltpu.VMEM((2, rows, rows), bf16)]
    scratch += [dma((n,)) for _ in range(4)] + [dma((n, 2)) for _ in range(8)] + [dma((n,)) for _ in range(4)]
    if backward:
        scratch += [pltpu.VMEM((4, rows, hidden), f32) for _ in range(2)]
    out_shape = [jax.ShapeDtypeStruct((rows, model_width), bf16)]
    operands = [packed, w_in, w_out]
    if backward:
        operands.append(pre)
    else:
        out_shape.append(jax.ShapeDtypeStruct((4, rows, hidden), f32))
    return pl.pallas_call(
        functools.partial(moe_kernel, backward, ny, nz),
        out_shape=out_shape,
        in_specs=[vmem] * len(operands),
        out_specs=[vmem] * len(out_shape),
        scratch_shapes=scratch,
        name="moe_back" if backward else "moe_fore",
        compiler_params=pltpu.CompilerParams(
            collective_id=1 if backward else 0,
            has_side_effects=True,
            vmem_limit_bytes=56 * 1024 * 1024,
        ),
    )(*operands)


def gather_kernel(ny, nz, u, out, near, block, half_block, held, s_n, r_n, s_a, r_a, s_b, r_b, s_c, r_c):
    dpn = lax.axis_size("dp")
    x = lax.axis_index("dp")
    rank = lax.axis_index("expert")
    c = lax.rem(rank, CORES)
    z = lax.rem(lax.div(rank, CORES), nz)
    y = lax.div(rank, CORES * nz)
    side = ny
    near_count = dpn * CORES
    own_near = x * CORES + c
    first = z * (1 - c) + y * c
    second = y * (1 - c) + z * c

    def at_rank(first_at, second_at):
        y_at = second_at * (1 - c) + first_at * c
        z_at = first_at * (1 - c) + second_at * c
        return (x, (y_at * nz + z_at) * CORES + c)

    near_peers = []
    for k in range(1, near_count):
        peer = lax.rem(own_near + k, near_count)
        near_peers.append((lax.div(peer, CORES), (y * nz + z) * CORES + lax.rem(peer, CORES)))
    a_peers = [at_rank(lax.rem(first + k, side), second) for k in near_first(side)]
    right = at_rank(first, lax.rem(second + 1, side))
    left = at_rank(first, lax.rem(second + side - 1, side))
    sibling = (x, rank + 1 - 2 * c)
    ring = [right] if side == 2 else [right, left]
    greet(near_peers + a_peers + ring)

    for peer in near_peers:
        send(u, near.at[own_near], s_n.at[0], r_n.at[0], peer)
    near[own_near] = u[...]
    drain(near.at[pl.ds(0, near_count - 1)], r_n.at[0])
    for k in range(near_count):
        for m in range(2):
            block[m * near_count + k : m * near_count + k + 1, :] = near[k, m : m + 1, :]
    half_width = half_block.shape[1]
    half_block[...] = jnp.where(c == 0, block[:, :half_width], block[:, half_width:]).astype(jnp.bfloat16)
    held[c, second, first] = half_block[...]
    for peer in a_peers:
        send(half_block, held.at[c, second, first], s_a.at[0], r_a.at[0], peer)
    drain(held.at[c, second, pl.ds(0, side - 1)], r_a.at[0])

    def share(slab, k):
        send(slab, slab, s_c.at[k], r_c.at[k], sibling)

    share(held.at[c, second], 0)
    full = side // 2 - 1
    for i in range(full):
        r_slab = held.at[c, lax.rem(second + side - i, side)]
        l_slab = held.at[c, lax.rem(second + i, side)]
        send(r_slab, r_slab, s_b.at[i, 0], r_b.at[i, 0], right)
        send(l_slab, l_slab, s_b.at[i, 1], r_b.at[i, 1], left)
        for way, got in enumerate((second + side - i - 1, second + i + 1)):
            slab = held.at[c, lax.rem(got, side)]
            drain(slab, r_b.at[i, way])
            share(slab, 1 + 2 * i + way)
    parts = (pl.ds(0, side // 2), pl.ds(side // 2, side // 2))
    r_slab = held.at[c, lax.rem(second + side - full, side), parts[0]]
    l_slab = held.at[c, lax.rem(second + full, side), parts[1]]
    send(r_slab, r_slab, s_b.at[full, 0], r_b.at[full, 0], right)
    send(l_slab, l_slab, s_b.at[full, 1], r_b.at[full, 1], left)
    for way in range(2):
        slab = held.at[c, lax.rem(second + side // 2, side), parts[way]]
        drain(slab, r_b.at[full, way])
        share(slab, 1 + 2 * full + way)

    for k in range(1 + 2 * full):
        drain(held.at[0, 0], r_c.at[k])
    for way in range(2):
        drain(held.at[0, 0, parts[way]], r_c.at[1 + 2 * full + way])
    for b in range(side):
        for a in range(side):
            out[b * nz + a, :, :half_width] = held[0, b, a]
            out[a * nz + b, :, half_width:] = held[1, b, a]

    drain(near.at[pl.ds(0, near_count - 1)], s_n.at[0])
    drain(held.at[c, second, pl.ds(0, side - 1)], s_a.at[0])
    for i in range(full):
        for way in range(2):
            drain(held.at[0, 0], s_b.at[i, way])
    for way in range(2):
        drain(held.at[0, 0, parts[way]], s_b.at[full, way])
    for k in range(1 + 2 * full):
        drain(held.at[0, 0], s_c.at[k])
    for way in range(2):
        drain(held.at[0, 0, parts[way]], s_c.at[1 + 2 * full + way])


def gather_call(experts, u):
    ny, nz = chip_sides(experts)
    side = ny
    model_width = u.shape[1]
    near_count = lax.axis_size("dp") * CORES
    rows = 2 * near_count
    steps = side // 2
    dma = pltpu.SemaphoreType.DMA
    vmem = pl.BlockSpec(memory_space=pltpu.VMEM)
    return pl.pallas_call(
        functools.partial(gather_kernel, ny, nz),
        out_shape=jax.ShapeDtypeStruct((ny * nz, rows, model_width), jnp.bfloat16),
        in_specs=[vmem],
        out_specs=vmem,
        scratch_shapes=[
            pltpu.VMEM((near_count, 2, model_width), jnp.float32),
            pltpu.VMEM((rows, model_width), jnp.float32),
            pltpu.VMEM((rows, model_width // 2), jnp.bfloat16),
            pltpu.VMEM((2, side, side, rows, model_width // 2), jnp.bfloat16),
            dma((1,)),
            dma((1,)),
            dma((1,)),
            dma((1,)),
            dma((steps, 2)),
            dma((steps, 2)),
            dma((2 * steps + 1,)),
            dma((2 * steps + 1,)),
        ],
        name="gather_units",
        compiler_params=pltpu.CompilerParams(
            collective_id=2, has_side_effects=True, vmem_limit_bytes=48 * 1024 * 1024
        ),
    )(u)


def local(tokens, ln_gain, w_router, w_in, w_out, expert_ids, keep, slots, logit_scale):
    pairs_dev, row_width, model_width = tokens.shape
    seq_len = row_width // 2
    token_count = pairs_dev * row_width
    dp_count = lax.axis_size("dp")
    experts = w_router.shape[1]
    capacity = max(2, 2 * token_count // experts)
    score_scale = logit_scale[0]
    rows_in = tokens.reshape(token_count, model_width).astype(jnp.float32)
    normed, norm_pull = jax.vjp(lambda values: layer_norm(values, ln_gain), rows_in)
    normed_b = normed.astype(jnp.bfloat16)
    routed = expert_ids.reshape(token_count)
    keep_flat = keep.reshape(token_count)
    keep_f = keep_flat.astype(jnp.float32)
    target = routed * capacity + slots.reshape(token_count)
    slot_iota = lax.broadcasted_iota(jnp.int32, (experts * capacity, token_count), 0)
    slot_table = ((slot_iota == target[None, :]) & (keep_flat[None, :] == 1)).astype(jnp.bfloat16)
    choose = (lax.broadcasted_iota(jnp.int32, (token_count, experts), 1) == routed[:, None]).astype(
        jnp.float32
    )
    logits = jnp.dot(normed_b, w_router, preferred_element_type=jnp.float32)
    expo = jnp.exp(logits)
    probs = expo / jnp.sum(expo, 1, keepdims=True)
    gate_val = jnp.sum(probs * choose, 1)
    packed = jnp.dot(slot_table, normed_b, preferred_element_type=jnp.float32).astype(jnp.bfloat16)
    expert_out, pre_act = moe_call(False, experts, packed, w_in[0], w_out[0])
    moe_rows = from_slots(slot_table, expert_out)
    mixed_rows = rows_in + (keep_f * gate_val)[:, None] * moe_rows
    pooled = jnp.mean(mixed_rows.reshape(pairs_dev, 2, seq_len, model_width), 2)
    unit_emb, unit_pull = jax.vjp(unit_rows, pooled)
    unit_b = unit_emb.astype(jnp.bfloat16)
    everyone = gather_call(experts, unit_b[0].astype(jnp.float32))
    near_count = dp_count * CORES
    images_all = everyone[:, :near_count].reshape(-1, model_width)
    texts_all = everyone[:, near_count:].reshape(-1, model_width)
    pair_count = images_all.shape[0]
    rank = lax.axis_index("expert")
    first_pair = (rank // CORES) * near_count + lax.axis_index("dp") * CORES + rank % CORES
    row_scores = score_scale * jnp.einsum(
        "pd,qd->pq", unit_b[:, 0], texts_all, preferred_element_type=jnp.float32
    )
    col_scores = score_scale * jnp.einsum(
        "pd,qd->pq", unit_b[:, 1], images_all, preferred_element_type=jnp.float32
    )
    all_scores = score_scale * jnp.einsum(
        "id,jd->ij", images_all, texts_all, preferred_element_type=jnp.float32
    )
    row_tot = jax.nn.logsumexp(all_scores, 1)
    col_tot = jax.nn.logsumexp(all_scores, 0)
    row_mine = lax.dynamic_slice_in_dim(row_tot, first_pair, pairs_dev)
    col_mine = lax.dynamic_slice_in_dim(col_tot, first_pair, pairs_dev)
    column_iota = lax.broadcasted_iota(jnp.int32, (pairs_dev, pair_count), 1)
    own_column = first_pair + lax.broadcasted_iota(jnp.int32, (pairs_dev, pair_count), 0)
    diag_mask = (column_iota == own_column).astype(jnp.float32)
    diag_score = jnp.sum(row_scores * diag_mask, 1)
    pair_loss = (row_mine + col_mine - 2.0 * diag_score) * 0.5
    weight_img = (
        (jnp.exp(row_scores - row_mine[:, None]) + jnp.exp(row_scores - col_tot[None, :])) * 0.5
        - diag_mask
    ).astype(jnp.bfloat16)
    weight_txt = (
        (jnp.exp(col_scores - row_tot[None, :]) + jnp.exp(col_scores - col_mine[:, None])) * 0.5
        - diag_mask
    ).astype(jnp.bfloat16)
    d_images = score_scale * jnp.dot(weight_img, texts_all, preferred_element_type=jnp.float32)
    d_texts = score_scale * jnp.dot(weight_txt, images_all, preferred_element_type=jnp.float32)
    d_pooled = unit_pull(jnp.stack([d_images, d_texts], 1))[0]
    d_mixed = jnp.broadcast_to(
        d_pooled[:, :, None, :] / seq_len, (pairs_dev, 2, seq_len, model_width)
    ).reshape(token_count, model_width)
    d_moe = ((keep_f * gate_val)[:, None] * d_mixed).astype(jnp.bfloat16)
    d_packed = jnp.dot(slot_table, d_moe, preferred_element_type=jnp.float32).astype(jnp.bfloat16)
    d_back = moe_call(True, experts, d_packed, w_in[0], w_out[0], pre_act)[0]
    d_normed_moe = from_slots(slot_table, d_back)
    d_gate = keep_f * jnp.sum(d_mixed * moe_rows, 1) * gate_val
    d_logit = d_gate[:, None] * (choose - probs)
    router_part = jnp.dot(d_logit, w_router.astype(jnp.float32).T, precision=lax.Precision.HIGHEST)
    d_normed = d_normed_moe + router_part
    d_tokens = d_mixed + norm_pull(d_normed)[0]
    tokens_grad = (d_tokens * (128.0 * seq_len / score_scale)).astype(jnp.bfloat16)
    return (pair_loss, tokens_grad.reshape(pairs_dev, row_width, model_width))


def solution(mesh):
    in_specs = (
        P(("dp", "expert"), None, None),
        P(),
        P(),
        P("expert", None, "dp"),
        P("expert", "dp", None),
        P(("dp", "expert"), None),
        P(("dp", "expert"), None),
        P(("dp", "expert"), None),
        P(),
    )
    out_specs = (P(("dp", "expert")), P(("dp", "expert"), None, None))
    return jax.shard_map(local, mesh=mesh, in_specs=in_specs, out_specs=out_specs, check_vma=False)
```

```python
import functools
import math

import jax
import jax.numpy as jnp
import numpy as np
from jax import lax
from jax.experimental import pallas as pl
from jax.experimental.pallas import tpu as pltpu
from jax.sharding import PartitionSpec as P

MESH = pl.DeviceIdType.MESH
norm_eps = 1e-06
WIDTHS = (256, 256, 256, 256, 384)
SIDE = 128
AWAY = (0, 3, 1, 2)
CORES = 2
SLOTS = 2


def activation(values):
    return 0.5 * values * (1.0 + lax.erf(values * (0.5**0.5)))


def activation_slope(values):
    bell = jnp.exp(-0.5 * values * values) * 0.3989422804014327
    return 0.5 * (1.0 + lax.erf(values * (0.5**0.5))) + values * bell


def layer_norm(matrix_rows, ln_gain):
    centered = matrix_rows - jnp.mean(matrix_rows, -1, keepdims=True)
    variance = jnp.mean(centered * centered, -1, keepdims=True)
    return centered * lax.rsqrt(variance + norm_eps) * ln_gain.astype(jnp.float32)


def chip_sides(experts):
    chips = experts // CORES
    side = 1
    while side * side < chips:
        side *= 2
    return side, chips // side


def near_first(count):
    offsets = []
    for step in range(1, count // 2 + 1):
        offsets.append(step)
        if count - step != step:
            offsets.append(count - step)
    return offsets


def send(src, dst, send_sem, recv_sem, device):
    pltpu.make_async_remote_copy(
        src_ref=src,
        dst_ref=dst,
        send_sem=send_sem,
        recv_sem=recv_sem,
        device_id=device,
        device_id_type=MESH,
    ).start()


def drain(ref, sem):
    pltpu.make_async_copy(ref, ref, sem).wait()


def greet(peers):
    barrier = pltpu.get_barrier_semaphore()
    for peer in peers:
        pl.semaphore_signal(barrier, inc=1, device_id=peer, device_id_type=MESH)
    pl.semaphore_wait(barrier, len(peers))


def from_slots(slot_table, matrix_rows):
    return jnp.einsum("st,sd->td", slot_table, matrix_rows, preferred_element_type=jnp.float32)


def selector(sizes, source):
    count = math.prod(sizes)
    place = np.arange(count)
    digits = np.unravel_index(place, sizes)
    table = np.zeros((count, count), np.float32)
    table[place, source(*digits)] = 1.0
    return jnp.asarray(table, jnp.bfloat16)


def move_rows(table, values):
    return jnp.dot(table, values, preferred_element_type=jnp.float32).astype(jnp.bfloat16)


def spans(model_width):
    widths = WIDTHS
    if sum(widths) != model_width + SIDE:
        widths = (model_width // 2, model_width - model_width // 2 + SIDE)
    return [(sum(widths[:t]), widths[t]) for t in range(len(widths))]


def by_slab(rows, slab, blocks, step):
    def body(i, carry):
        for b in blocks:
            step(b, i, pl.ds(pl.multiple_of(i * slab, slab), slab))
        return carry

    lax.fori_loop(0, rows // slab, body, 0)


class Place:
    def __init__(self, ny, nz):
        self.ny, self.nz = ny, nz
        self.nzc = nz * CORES
        self.yb, self.zb = self.nzc * SLOTS, ny * SLOTS
        self.dpn = lax.axis_size("dp")
        self.x = lax.axis_index("dp")
        self.rank = lax.axis_index("expert")
        self.y, self.zc = lax.div(self.rank, self.nzc), lax.rem(self.rank, self.nzc)
        self.c = lax.rem(self.rank, CORES)
        self.z = lax.div(self.zc, CORES)
        self.right = (lax.rem(self.x + 1, self.dpn), self.rank)
        self.left = (lax.rem(self.x + self.dpn - 1, self.dpn), self.rank)
        self.first = self.y * (1 - self.c) + self.z * self.c
        self.second = self.z * (1 - self.c) + self.y * self.c
        self.sibling = (self.x, self.rank + 1 - 2 * self.c)
        self.y_peers = [lax.rem(self.y + k, ny) for k in near_first(ny)]
        self.z_peers = [lax.rem(self.zc + k, self.nzc) for k in near_first(self.nzc)]

    def at_y(self, peer):
        return (self.x, peer * self.nzc + self.zc)

    def at_z(self, peer):
        return (self.x, self.y * self.nzc + peer)

    def at_grid(self, first, second):
        c = self.c
        y_at = first * (1 - c) + second * c
        z_at = second * (1 - c) + first * c
        return (self.x, y_at * self.nzc + z_at * CORES + c)

    def at_near(self, b, core):
        return (lax.rem(self.x + AWAY[b], self.dpn), self.y * self.nzc + self.z * CORES + core)

    def y_block(self, index):
        return pl.ds(pl.multiple_of(index * self.yb, self.yb), self.yb)

    def z_block(self, index):
        return pl.ds(pl.multiple_of(index * self.zb, self.zb), self.zb)


def fore_kernel(ny, nz, spread, scale, *refs):
    src, u, w_in_far, w_out_far, perm, perm_small, perm_x, out, slope, hid, side = refs[:11]
    n = len(spread)
    bufs = [refs[11 + 6 * t : 17 + 6 * t] for t in range(n)]
    at = 11 + 6 * n
    w_in, w_out, acc, hc, hp, po, sib_out, sib_in, st, got, sums, st_b, got_b = refs[at : at + 13]
    near, block, st_c, got_c, half_block, held = refs[at + 13 : at + 19]
    s_y, r_y, s_z, r_z, s_x, r_x, s_o, r_o, s_d, r_d, s_f, r_f, s_g, r_g = refs[at + 19 : at + 33]
    s_b, r_b, s_c, r_c, load = refs[at + 33 :]
    p = Place(ny, nz)
    rows = acc.shape[1]
    half = rows // 2
    top, low = pl.ds(0, half), pl.ds(half, half)
    yb, zb = p.yb, p.zb
    half_width = po.shape[2]
    model_width = 2 * half_width

    pltpu.make_async_copy(w_in_far, w_in, load.at[0]).start()
    pltpu.make_async_copy(w_out_far, w_out, load.at[1]).start()
    others = [p.at_near(b, core) for b in range(1, 4) for core in range(CORES)]
    greet([p.at_y(peer) for peer in p.y_peers] + [p.at_z(peer) for peer in p.z_peers] + others)

    for t, (start, width) in enumerate(spread):
        for peer in p.y_peers:
            send(
                src.at[p.y_block(peer), pl.ds(start, width)],
                bufs[t][0].at[p.y_block(p.y)],
                s_y.at[t],
                r_y.at[t],
                p.at_y(peer),
            )

    own_near = p.x * CORES + p.c
    near_count = 4 * CORES
    for peer in others + [p.sibling]:
        send(u, near.at[own_near], s_g.at[0], r_g.at[0], peer)
    near[own_near] = u[...]

    def stage_z(t):
        ybuf, zsend, zbuf = bufs[t][:3]
        start, width = spread[t]
        ybuf[p.y_block(p.y), :] = src[p.y_block(p.y), start : start + width]
        drain(ybuf.at[pl.ds(0, rows - yb)], r_y.at[t])
        zsend[...] = move_rows(perm[0], ybuf[...])
        for peer in p.z_peers:
            send(zsend.at[p.z_block(peer)], zbuf.at[p.z_block(p.zc)], s_z.at[t], r_z.at[t], p.at_z(peer))
        zbuf[p.z_block(p.zc), :] = zsend[p.z_block(p.zc), :]

    def stage_x(t):
        zbuf, xl, xr = bufs[t][2:5]
        drain(zbuf.at[pl.ds(0, rows - zb)], r_z.at[t])
        send(zbuf, xl, s_x.at[t, 0], r_x.at[t, 0], p.right)
        send(zbuf, xr, s_x.at[t, 1], r_x.at[t, 1], p.left)

    def stage_forward(t):
        xl, xr, xo = bufs[t][3:6]
        drain(xl, r_x.at[t, 0])
        send(xl.at[top], xo.at[top], s_o.at[t, 0], r_o.at[t, 0], p.right)
        drain(xr, r_x.at[t, 1])
        send(xr.at[low], xo.at[low], s_o.at[t, 1], r_o.at[t, 1], p.left)

    def stage_in(t, b):
        start, width = spread[t]
        depth = min(start + width, model_width) - start
        values = bufs[t][2 + b]
        part = jnp.dot(values[:, :depth], w_in[start : start + depth, :], preferred_element_type=jnp.float32)
        acc[b] = part if t == 0 else acc[b] + part
        if t == n - 1:
            side[b] = values[:, depth:]

    def await_far(t):
        xo = bufs[t][5]
        drain(xo.at[top], r_o.at[t, 0])
        drain(xo.at[low], r_o.at[t, 1])

    for t in range(n + 2):
        if t < n:
            stage_z(t)
        if 0 <= t - 1 < n:
            stage_x(t - 1)
        if 0 <= t - 2 < n:
            stage_forward(t - 2)
        if t == 2:
            pltpu.make_async_copy(w_in_far, w_in, load.at[0]).wait()
        if 0 <= t - 3 < n - 1:
            await_far(t - 3)
            for b in range(4):
                stage_in(t - 3, b)

    def hidden_step(b, i, rows_at):
        values = activation(acc[b, rows_at, :])
        hid[b, rows_at, :] = values.astype(jnp.bfloat16)
        gates = side[b, rows_at, :].astype(jnp.float32)
        image = values * (gates[:, 0:1] + gates[:, 1:2])
        text = values * (gates[:, 2:3] + gates[:, 3:4])
        both = jnp.concatenate([image[:ny] + image[ny:], text[:ny] + text[ny:]], 0)
        hc[b, rows_at, :] = both.astype(jnp.bfloat16)

    def half_cols(core):
        return pl.ds(pl.multiple_of(core * half_width, half_width), half_width)

    other = 1 - p.c
    line = [lax.rem(p.first + k, ny) for k in near_first(ny)]

    def stage_line(b):
        drain(sib_in.at[b], r_d.at[b])
        st[b] = (po[b] + sib_in[b].astype(jnp.float32)).astype(jnp.bfloat16)
        for peer in line:
            send(
                st.at[b, p.y_block(peer)], got.at[b, p.first], s_f.at[b], r_f.at[b], p.at_grid(peer, p.second)
            )
        got[b, p.first] = st[b, p.y_block(p.first), :]

    pltpu.make_async_copy(w_out_far, w_out, load.at[1]).wait()
    for b in range(4):
        if b == 3:
            await_far(n - 1)
        stage_in(n - 1, b)
        by_slab(rows, zb, [b], hidden_step)
        hp[0] = move_rows(perm[1 + other], hc[b])
        sib_out[b] = jnp.dot(hp[0], w_out[:, half_cols(other)], preferred_element_type=jnp.float32).astype(
            jnp.bfloat16
        )
        send(sib_out.at[b], sib_in.at[b], s_d.at[b], r_d.at[b], p.sibling)
        hp[1] = move_rows(perm[1 + p.c], hc[b])
        po[b] = jnp.dot(hp[1], w_out[:, half_cols(p.c)], preferred_element_type=jnp.float32)
        if b > 0:
            stage_line(b - 1)
    stage_line(3)

    def slope_step(b, i, rows_at):
        slope[b, rows_at, :] = activation_slope(acc[b, rows_at, :])

    by_slab(rows, zb, range(2), slope_step)

    for b in range(4):
        drain(got.at[b, pl.ds(0, ny - 1)], r_f.at[b])
        total = got[b, 0].astype(jnp.float32)
        for k in range(1, ny):
            total = total + got[b, k].astype(jnp.float32)
        sums[b * yb : (b + 1) * yb, :] = total.astype(jnp.bfloat16)
    st_b[...] = move_rows(perm_small[...], sums[...])
    cut = 4 * CORES * 2

    def cut_block(index):
        return pl.ds(pl.multiple_of(index * cut, cut), cut)

    for k in near_first(ny):
        peer = lax.rem(p.second + k, ny)
        send(st_b.at[cut_block(peer)], got_b.at[p.second], s_g.at[1], r_g.at[1], p.at_grid(p.first, peer))
    got_b[p.second] = st_b[cut_block(p.second), :]
    drain(got_b.at[pl.ds(0, ny - 1)], r_g.at[1])
    total = got_b[0].astype(jnp.float32)
    for k in range(1, ny):
        total = total + got_b[k].astype(jnp.float32)
    part_rows = CORES * 2
    for b in range(4):
        st_c[lax.rem(p.x + AWAY[b], 4)] = total[b * part_rows : (b + 1) * part_rows]
    for b in range(1, 4):
        send(st_c, got_c.at[p.x], s_g.at[2], r_g.at[2], p.at_near(b, p.c))
    got_c[p.x] = st_c[...]
    drain(near.at[pl.ds(0, near_count - 1)], r_g.at[0])
    for k in range(near_count):
        for m in range(2):
            block[m * near_count + k : m * near_count + k + 1, :] = near[k, m : m + 1, :]
    drain(got_c.at[pl.ds(0, 3)], r_g.at[2])
    total = got_c[0] + got_c[1] + got_c[2] + got_c[3]
    for k in range(near_count):
        for m in range(2):
            row = m * near_count + k
            half_sum = jnp.where(p.c == 0, block[row : row + 1, :half_width], block[row : row + 1, half_width:])
            block[row : row + 1, :half_width] = half_sum + total[k // CORES, k % CORES * 2 + m][None]
    half_block[...] = (block[:, :half_width] * scale).astype(jnp.bfloat16)

    c, side_len, second = p.c, ny, p.second
    held[c, second, p.first] = half_block[...]
    for peer in line:
        send(half_block, held.at[c, second, p.first], s_g.at[3], r_g.at[3], p.at_grid(peer, second))
    drain(held.at[c, second, pl.ds(0, side_len - 1)], r_g.at[3])

    def share(slab, k):
        send(slab, slab, s_c.at[k], r_c.at[k], p.sibling)

    share(held.at[c, second], 0)
    right = p.at_grid(p.first, lax.rem(second + 1, side_len))
    left = p.at_grid(p.first, lax.rem(second + side_len - 1, side_len))
    full = side_len // 2 - 1
    for i in range(full):
        r_slab = held.at[c, lax.rem(second + side_len - i, side_len)]
        l_slab = held.at[c, lax.rem(second + i, side_len)]
        send(r_slab, r_slab, s_b.at[i, 0], r_b.at[i, 0], right)
        send(l_slab, l_slab, s_b.at[i, 1], r_b.at[i, 1], left)
        if i == 0:
            by_slab(rows, zb, range(2, 4), slope_step)
        for way, here in enumerate((second + side_len - i - 1, second + i + 1)):
            slab = held.at[c, lax.rem(here, side_len)]
            drain(slab, r_b.at[i, way])
            share(slab, 1 + 2 * i + way)
    parts = (pl.ds(0, side_len // 2), pl.ds(side_len // 2, side_len // 2))
    r_slab = held.at[c, lax.rem(second + side_len - full, side_len), parts[0]]
    l_slab = held.at[c, lax.rem(second + full, side_len), parts[1]]
    send(r_slab, r_slab, s_b.at[full, 0], r_b.at[full, 0], right)
    send(l_slab, l_slab, s_b.at[full, 1], r_b.at[full, 1], left)
    if full == 0:
        by_slab(rows, zb, range(2, 4), slope_step)
    for way in range(2):
        slab = held.at[c, lax.rem(second + side_len // 2, side_len), parts[way]]
        drain(slab, r_b.at[full, way])
        share(slab, 1 + 2 * full + way)
    for k in range(1 + 2 * full):
        drain(held.at[0, 0], r_c.at[k])
    for way in range(2):
        drain(held.at[0, 0, parts[way]], r_c.at[1 + 2 * full + way])
    span = CORES * side_len
    for h in range(CORES):
        for z_at in range(side_len):
            slab = held[h, z_at] if h == 0 else held[h, :, z_at]
            moved = move_rows(perm_x[p.x], slab.reshape(side_len * 2 * near_count, half_width))
            for k in range(2 * 4):
                out[k // 4, k % 4, z_at * span : (z_at + 1) * span, h * half_width : (h + 1) * half_width] = moved[
                    k * span : (k + 1) * span
                ]

    for t in range(n):
        ybuf, zsend, zbuf, xl, xr, xo = bufs[t]
        drain(ybuf.at[pl.ds(0, rows - yb)], s_y.at[t])
        drain(zsend.at[pl.ds(0, rows - zb)], s_z.at[t])
        for way in range(2):
            drain(zbuf, s_x.at[t, way])
            drain(xo.at[top], s_o.at[t, way])
    for b in range(4):
        drain(sib_out.at[b], s_d.at[b])
        drain(got.at[b, pl.ds(0, ny - 1)], s_f.at[b])
    drain(near.at[pl.ds(0, near_count - 1)], s_g.at[0])
    drain(got_b.at[pl.ds(0, ny - 1)], s_g.at[1])
    drain(got_c.at[pl.ds(0, 3)], s_g.at[2])
    drain(held.at[0, 0, pl.ds(0, ny - 1)], s_g.at[3])
    for way in range(2):
        for i in range(full):
            drain(held.at[0, 0], s_b.at[i, way])
        drain(held.at[0, 0, parts[way]], s_b.at[full, way])
        drain(held.at[0, 0, parts[way]], s_c.at[1 + 2 * full + way])
    for k in range(1 + 2 * full):
        drain(held.at[0, 0], s_c.at[k])


def fore_call(experts, seq_len, packed, u, w_in, w_out):
    ny, nz = chip_sides(experts)
    rows = packed.shape[0]
    model_width, hidden = w_in.shape
    half_width = model_width // 2
    spread = spans(model_width)
    n = len(spread)
    yb, zb, cut = nz * CORES * SLOTS, ny * SLOTS, 4 * CORES * 2
    bf16, f32 = jnp.bfloat16, jnp.float32
    vmem = pl.BlockSpec(memory_space=pltpu.VMEM)
    far = pl.BlockSpec(memory_space=pl.ANY)
    dma = pltpu.SemaphoreType.DMA
    perm = jnp.stack(
        [
            selector((nz * CORES, SLOTS, ny), lambda zc, s, ys: ys * yb + zc * SLOTS + s),
            selector((ny, nz, CORES, 2), lambda ys, zs, cs, m: (zs * CORES + cs) * zb + m * ny + ys),
            selector((nz, ny, CORES, 2), lambda zs, ys, cs, m: (zs * CORES + cs) * zb + m * ny + ys),
        ]
    )
    perm_small = selector((ny, 4, CORES, 2), lambda second, b, cs, m: b * yb + second * 4 + cs * 2 + m)
    perm_x = jnp.stack(
        [
            selector(
                (2, 4, CORES, ny),
                lambda m, b, cs, ys: ys * cut + m * 4 * CORES + (x + np.array(AWAY)[b]) % 4 * CORES + cs,
            )
            for x in range(4)
        ]
    )
    scratch = [pltpu.VMEM((rows, width), bf16) for _, width in spread for _ in range(6)]
    scratch += [
        pltpu.VMEM(w_in.shape, bf16),
        pltpu.VMEM(w_out.shape, bf16),
        pltpu.VMEM((4, rows, hidden), f32),
        pltpu.VMEM((4, rows, hidden), bf16),
        pltpu.VMEM((2, rows, hidden), bf16),
        pltpu.VMEM((4, rows, half_width), f32),
        pltpu.VMEM((4, rows, half_width), bf16),
        pltpu.VMEM((4, rows, half_width), bf16),
        pltpu.VMEM((4, rows, half_width), bf16),
        pltpu.VMEM((4, ny, yb, half_width), bf16),
        pltpu.VMEM((4 * yb, half_width), bf16),
        pltpu.VMEM((4 * yb, half_width), bf16),
        pltpu.VMEM((ny, cut, half_width), bf16),
        pltpu.VMEM((4 * CORES, 2, model_width), f32),
        pltpu.VMEM((cut, model_width), f32),
        pltpu.VMEM((4, CORES * 2, half_width), f32),
        pltpu.VMEM((4, 4, CORES * 2, half_width), f32),
        pltpu.VMEM((cut, half_width), bf16),
        pltpu.VMEM((CORES, nz, ny, cut, half_width), bf16),
    ]
    steps = ny // 2
    scratch += [dma((n,)) for _ in range(4)] + [dma((n, 2)) for _ in range(4)]
    scratch += [dma((4,)) for _ in range(6)]
    scratch += [dma((steps, 2)) for _ in range(2)] + [dma((2 * steps + 1,)) for _ in range(2)] + [dma((2,))]
    return pl.pallas_call(
        functools.partial(fore_kernel, ny, nz, spread, 1.0 / seq_len),
        out_shape=[
            jax.ShapeDtypeStruct((2, 4, experts, model_width), bf16),
            jax.ShapeDtypeStruct((4, rows, hidden), f32),
            jax.ShapeDtypeStruct((4, rows, hidden), bf16),
            jax.ShapeDtypeStruct((4, rows, SIDE), bf16),
        ],
        in_specs=[vmem, vmem, far, far, vmem, vmem, vmem],
        out_specs=[vmem] * 4,
        scratch_shapes=scratch,
        name="moe_fore",
        compiler_params=pltpu.CompilerParams(
            collective_id=0, has_side_effects=True, vmem_limit_bytes=56 * 1024 * 1024
        ),
    )(packed, u, w_in, w_out, perm, perm_small, perm_x)


def back_kernel(ny, nz, spread, *refs):
    d_all, w_in_far, w_out, slope_far, hid_far, side, perm, out = refs[:8]
    n = len(spread)
    bufs = [refs[8 + 12 * t : 20 + 12 * t] for t in range(n)]
    at = 8 + 12 * n
    pulled, d_pre, d_gate, w_in, slope, hid = refs[at : at + 6]
    s_p, r_p, s_q, r_q, s_z, r_z, s_y, r_y, load = refs[at + 6 :]
    loads = [
        pltpu.make_async_copy(w_in_far, w_in, load.at[0]),
        pltpu.make_async_copy(slope_far, slope, load.at[1]),
        pltpu.make_async_copy(hid_far, hid, load.at[2]),
    ]
    for copy in (loads[1], loads[2], loads[0]):
        copy.start()
    p = Place(ny, nz)
    rows = slope_far.shape[1]
    half = rows // 2
    top, low = pl.ds(0, half), pl.ds(half, half)
    yb, zb = p.yb, p.zb
    model_width = w_in_far.shape[0]
    pairs = d_all.shape[1]

    greet(
        [p.at_y(peer) for peer in p.y_peers] + [p.at_z(peer) for peer in p.z_peers] + [p.right, p.left]
    )

    def pull(b):
        part = pl.ds(b * (pairs // 4), pairs // 4)
        for m in range(2):
            pulled[m, part, :] = lax.dot_general(
                d_all[m, part, :], w_out[...], (((1,), (1,)), ((), ())), preferred_element_type=jnp.float32
            )

    def pre_step(b, i, rows_at):
        pair_at = pl.ds(pl.multiple_of(b * (pairs // 4) + i * ny, ny), ny)
        gates = side[b, rows_at, :].astype(jnp.float32)
        image = pulled[0, pair_at, :]
        text = pulled[1, pair_at, :]
        d_act = jnp.concatenate([image, image], 0) * (gates[:, 0:1] + gates[:, 1:2])
        d_act = d_act + jnp.concatenate([text, text], 0) * (gates[:, 2:3] + gates[:, 3:4])
        d_pre[b, rows_at, :] = (d_act * slope[b, rows_at, :]).astype(jnp.bfloat16)
        value = jnp.sum(d_act * hid[b, rows_at, :].astype(jnp.float32), 1, keepdims=True)
        high = value.astype(jnp.bfloat16).astype(jnp.float32)
        lane = lax.broadcasted_iota(jnp.int32, (zb, SIDE), 1)
        d_gate[b, rows_at, :] = jnp.where(
            lane == 2 * p.x, high, jnp.where(lane == 2 * p.x + 1, value - high, 0.0)
        )

    def product_out(b, t):
        start, width = spread[t]
        depth = min(start + width, model_width) - start
        part = lax.dot_general(
            d_pre[b], w_in[start : start + depth, :], (((1,), (1,)), ((), ())), preferred_element_type=jnp.float32
        )
        if t == n - 1:
            part = jnp.concatenate([part, d_gate[b]], 1)
        return part

    def stage_far(t):
        so, sr, sl, ol, orr = bufs[t][:5]
        so[...] = product_out(3, t).astype(jnp.bfloat16)
        send(so.at[top], ol, s_p.at[t, 0], r_p.at[t, 0], p.right)
        send(so.at[low], orr, s_p.at[t, 1], r_p.at[t, 1], p.left)

    def stage_near(t):
        so, sr, sl, ol, orr, fl, fr, zs, zr, ys, yr, own = bufs[t]
        part = product_out(2, t)
        sr[half:, :] = part[half:].astype(jnp.bfloat16)
        drain(ol, r_p.at[t, 0])
        sr[:half, :] = (part[:half] + ol[...].astype(jnp.float32)).astype(jnp.bfloat16)
        send(sr, fl, s_q.at[t, 0], r_q.at[t, 0], p.right)
        part = product_out(1, t)
        sl[:half, :] = part[:half].astype(jnp.bfloat16)
        drain(orr, r_p.at[t, 1])
        sl[half:, :] = (part[half:] + orr[...].astype(jnp.float32)).astype(jnp.bfloat16)
        send(sl, fr, s_q.at[t, 1], r_q.at[t, 1], p.left)
        own[...] = product_out(0, t)

    def stage_back_z(t):
        so, sr, sl, ol, orr, fl, fr, zs, zr, ys, yr, own = bufs[t]
        drain(fl, r_q.at[t, 0])
        drain(fr, r_q.at[t, 1])
        zs[...] = (own[...] + fl[...].astype(jnp.float32) + fr[...].astype(jnp.float32)).astype(jnp.bfloat16)
        for peer in p.z_peers:
            send(zs.at[p.z_block(peer)], zr.at[p.z_block(p.zc)], s_z.at[t], r_z.at[t], p.at_z(peer))
        zr[p.z_block(p.zc), :] = zs[p.z_block(p.zc), :]

    def stage_back_y(t):
        zr, ys, yr = bufs[t][8:11]
        drain(zr.at[pl.ds(0, rows - zb)], r_z.at[t])
        ys[...] = move_rows(perm[...], zr[...])
        for peer in p.y_peers:
            send(ys.at[p.y_block(peer)], yr.at[p.y_block(p.y)], s_y.at[t], r_y.at[t], p.at_y(peer))
        yr[p.y_block(p.y), :] = ys[p.y_block(p.y), :]

    def stage_store(t):
        yr = bufs[t][10]
        start, width = spread[t]
        drain(yr.at[pl.ds(0, rows - yb)], r_y.at[t])
        out[:, start : start + width] = yr[...]

    pull(3)
    loads[1].wait()
    loads[2].wait()
    by_slab(rows, zb, [3], pre_step)
    loads[0].wait()
    for t in range(n):
        stage_far(t)
    for b in range(3):
        pull(b)
    by_slab(rows, zb, range(3), pre_step)
    for t in range(n + 3):
        if t < n:
            stage_near(t)
        if 0 <= t - 1 < n:
            stage_back_z(t - 1)
        if 0 <= t - 2 < n:
            stage_back_y(t - 2)
        if 0 <= t - 3 < n:
            stage_store(t - 3)

    for t in range(n):
        so, sr, sl, ol, orr, fl, fr, zs, zr, ys, yr, own = bufs[t]
        drain(zs.at[pl.ds(0, rows - zb)], s_z.at[t])
        drain(ys.at[pl.ds(0, rows - yb)], s_y.at[t])
        for way in range(2):
            drain(so.at[top], s_p.at[t, way])
            drain(sr, s_q.at[t, way])


def back_call(experts, d_all, w_in, w_out, slope, hid, side):
    ny, nz = chip_sides(experts)
    rows = slope.shape[1]
    model_width, hidden = w_in.shape
    spread = spans(model_width)
    n = len(spread)
    half = rows // 2
    bf16, f32 = jnp.bfloat16, jnp.float32
    vmem = pl.BlockSpec(memory_space=pltpu.VMEM)
    dma = pltpu.SemaphoreType.DMA
    scratch = []
    for _, width in spread:
        scratch += [pltpu.VMEM((rows, width), bf16) for _ in range(3)]
        scratch += [pltpu.VMEM((half, width), bf16) for _ in range(2)]
        scratch += [pltpu.VMEM((rows, width), bf16) for _ in range(6)]
        scratch += [pltpu.VMEM((rows, width), f32)]
    scratch += [
        pltpu.VMEM((2, d_all.shape[1], hidden), f32),
        pltpu.VMEM((4, rows, hidden), bf16),
        pltpu.VMEM((4, rows, SIDE), f32),
        pltpu.VMEM(w_in.shape, bf16),
        pltpu.VMEM(slope.shape, f32),
        pltpu.VMEM(hid.shape, bf16),
    ]
    scratch += [dma((n, 2)) for _ in range(4)] + [dma((n,)) for _ in range(4)] + [dma((3,))]
    yb, zb = nz * CORES * SLOTS, ny * SLOTS
    perm = selector((ny, nz * CORES, SLOTS), lambda ys, zc, s: zc * zb + s * ny + ys)
    far = pl.BlockSpec(memory_space=pl.ANY)
    return pl.pallas_call(
        functools.partial(back_kernel, ny, nz, spread),
        out_shape=jax.ShapeDtypeStruct((rows, model_width + SIDE), bf16),
        in_specs=[vmem, far, vmem, far, far, vmem, vmem],
        out_specs=vmem,
        scratch_shapes=scratch,
        name="moe_back",
        compiler_params=pltpu.CompilerParams(
            collective_id=1, has_side_effects=True, vmem_limit_bytes=56 * 1024 * 1024
        ),
    )(d_all, w_in, w_out, slope, hid, side, perm)


def local(tokens, ln_gain, w_router, w_in, w_out, expert_ids, keep, slots, logit_scale):
    pairs_dev, row_width, model_width = tokens.shape
    seq_len = row_width // 2
    token_count = pairs_dev * row_width
    experts = w_router.shape[1]
    capacity = SLOTS
    score_scale = logit_scale[0]
    rows_in = tokens.reshape(token_count, model_width).astype(jnp.float32)
    normed, norm_pull = jax.vjp(lambda values: layer_norm(values, ln_gain), rows_in)
    normed_b = normed.astype(jnp.bfloat16)
    routed = expert_ids.reshape(token_count)
    keep_flat = keep.reshape(token_count)
    target = routed * capacity + slots.reshape(token_count)
    slot_iota = lax.broadcasted_iota(jnp.int32, (experts * capacity, token_count), 0)
    slot_table = ((slot_iota == target[None, :]) & (keep_flat[None, :] == 1)).astype(jnp.bfloat16)
    choose = (lax.broadcasted_iota(jnp.int32, (token_count, experts), 1) == routed[:, None]).astype(
        jnp.float32
    )
    logits = jnp.dot(normed_b, w_router, preferred_element_type=jnp.float32)
    expo = jnp.exp(logits)
    probs = expo / jnp.sum(expo, 1, keepdims=True)
    gate_val = jnp.sum(probs * choose, 1, keepdims=True)
    high = gate_val.astype(jnp.bfloat16).astype(jnp.float32)
    lane = lax.broadcasted_iota(jnp.int32, (token_count, SIDE), 1)
    modality = lax.broadcasted_iota(jnp.int32, (token_count, SIDE), 0) // seq_len
    gate_side = jnp.where(
        lane == 2 * modality, high, jnp.where(lane == 2 * modality + 1, gate_val - high, 0.0)
    ).astype(jnp.bfloat16)
    packed = jnp.dot(
        slot_table, jnp.concatenate([normed_b, gate_side], 1), preferred_element_type=jnp.float32
    ).astype(jnp.bfloat16)
    token_sums = jnp.sum(rows_in.reshape(2, seq_len, model_width), 1)
    everyone, slope, hid, side = fore_call(experts, seq_len, packed, token_sums, w_in[0], w_out[0])
    everyone = everyone.reshape(2, -1, model_width)
    pair_count = everyone.shape[1]
    all_f = everyone.astype(jnp.float32)
    inverse = lax.rsqrt(jnp.sum(all_f * all_f, -1) + norm_eps)
    ny, nz = chip_sides(experts)
    rank = lax.axis_index("expert")
    own_index = (rank % (nz * CORES)) * ny + rank // (nz * CORES)
    scores = (
        jnp.einsum("id,jd->ij", everyone[0], everyone[1], preferred_element_type=jnp.float32)
        * (score_scale * inverse[0])[:, None]
        * inverse[1][None, :]
    )
    row_tot = jax.nn.logsumexp(scores, 1)
    col_tot = jax.nn.logsumexp(scores, 0)
    row_iota = lax.broadcasted_iota(jnp.int32, (pair_count, pair_count), 0)
    eye = (row_iota == lax.broadcasted_iota(jnp.int32, (pair_count, pair_count), 1)).astype(jnp.float32)
    diag_score = jnp.sum(scores * eye, 1)
    losses = (row_tot + col_tot - 2.0 * diag_score) * 0.5
    pair_loss = lax.dynamic_slice_in_dim(losses, own_index, pairs_dev)
    weights = (jnp.exp(scores - row_tot[:, None]) + jnp.exp(scores - col_tot[None, :])) * 0.5 - eye
    d_images = jnp.dot(
        (weights * inverse[1][None, :]).astype(jnp.bfloat16), everyone[1], preferred_element_type=jnp.float32
    )
    d_texts = lax.dot_general(
        (weights * inverse[0][:, None]).astype(jnp.bfloat16),
        everyone[0],
        (((0,), (0,)), ((), ())),
        preferred_element_type=jnp.float32,
    )
    d_units = jnp.stack([d_images, d_texts])
    units = all_f * inverse[:, :, None]
    along = jnp.sum(d_units * units, -1, keepdims=True)
    d_pooled = (d_units - units * along) * (inverse * (score_scale / seq_len))[:, :, None]
    d_own = lax.dynamic_slice_in_dim(d_pooled, own_index, pairs_dev, 1)
    d_mixed = jnp.broadcast_to(d_own, (2, seq_len, model_width)).reshape(token_count, model_width)
    d_back = back_call(experts, d_pooled.astype(jnp.bfloat16), w_in[0], w_out[0], slope, hid, side)
    d_slots = jnp.einsum("st,sd->td", slot_table, d_back, preferred_element_type=jnp.float32)
    d_gate = jnp.sum(d_slots[:, model_width : model_width + 8], 1)
    d_logit = d_gate[:, None] * (choose - probs)
    router_part = jnp.dot(d_logit, w_router.astype(jnp.float32).T, precision=lax.Precision.HIGHEST)
    d_normed = d_slots[:, :model_width] + router_part
    d_tokens = d_mixed + norm_pull(d_normed)[0]
    tokens_grad = (d_tokens * (128.0 * seq_len / score_scale)).astype(jnp.bfloat16)
    return (pair_loss, tokens_grad.reshape(pairs_dev, row_width, model_width))


def solution(mesh):
    in_specs = (
        P(("dp", "expert"), None, None),
        P(),
        P(),
        P("expert", None, "dp"),
        P("expert", "dp", None),
        P(("dp", "expert"), None),
        P(("dp", "expert"), None),
        P(("dp", "expert"), None),
        P(),
    )
    out_specs = (P(("dp", "expert")), P(("dp", "expert"), None, None))
    return jax.shard_map(local, mesh=mesh, in_specs=in_specs, out_specs=out_specs, check_vma=False)
```

```python
import functools
import math

import jax
import jax.numpy as jnp
import numpy as np
from jax import lax
from jax.experimental import pallas as pl
from jax.experimental.pallas import tpu as pltpu
from jax.sharding import PartitionSpec as P

MESH = pl.DeviceIdType.MESH
norm_eps = 1e-06
WIDTHS_IN = (256, 384, 384, 384)
WIDTHS_OUT = (384, 384, 384, 256)
SIDE = 128
AWAY = (0, 3, 1, 2)
CORES = 2
SLOTS = 2


def activation(values):
    return 0.5 * values * (1.0 + lax.erf(values * (0.5**0.5)))


def activation_slope(values):
    bell = jnp.exp(-0.5 * values * values) * 0.3989422804014327
    return 0.5 * (1.0 + lax.erf(values * (0.5**0.5))) + values * bell


def layer_norm(matrix_rows, ln_gain):
    centered = matrix_rows - jnp.mean(matrix_rows, -1, keepdims=True)
    variance = jnp.mean(centered * centered, -1, keepdims=True)
    return centered * lax.rsqrt(variance + norm_eps) * ln_gain.astype(jnp.float32)


def chip_sides(experts):
    chips = experts // CORES
    side = 1
    while side * side < chips:
        side *= 2
    return side, chips // side


def near_first(count):
    offsets = []
    for step in range(1, count // 2 + 1):
        offsets.append(step)
        if count - step != step:
            offsets.append(count - step)
    return offsets


def send(src, dst, send_sem, recv_sem, device):
    pltpu.make_async_remote_copy(
        src_ref=src,
        dst_ref=dst,
        send_sem=send_sem,
        recv_sem=recv_sem,
        device_id=device,
        device_id_type=MESH,
    ).start()


def drain(ref, sem):
    pltpu.make_async_copy(ref, ref, sem).wait()


def greet(peers):
    barrier = pltpu.get_barrier_semaphore()
    for peer in peers:
        pl.semaphore_signal(barrier, inc=1, device_id=peer, device_id_type=MESH)
    pl.semaphore_wait(barrier, len(peers))


def from_slots(slot_table, matrix_rows):
    return jnp.einsum("st,sd->td", slot_table, matrix_rows, preferred_element_type=jnp.float32)


def selector(sizes, source):
    count = math.prod(sizes)
    place = np.arange(count)
    digits = np.unravel_index(place, sizes)
    table = np.zeros((count, count), np.float32)
    table[place, source(*digits)] = 1.0
    return jnp.asarray(table, jnp.bfloat16)


def move_rows(table, values):
    return jnp.dot(table, values, preferred_element_type=jnp.float32).astype(jnp.bfloat16)


def spans(model_width, widths):
    if sum(widths) != model_width + SIDE:
        widths = (model_width // 2, model_width - model_width // 2 + SIDE)
    return [(sum(widths[:t]), widths[t]) for t in range(len(widths))]


def by_slab(rows, slab, blocks, step):
    def body(i, carry):
        for b in blocks:
            step(b, i, pl.ds(pl.multiple_of(i * slab, slab), slab))
        return carry

    lax.fori_loop(0, rows // slab, body, 0)


class Place:
    def __init__(self, ny, nz):
        self.ny, self.nz = ny, nz
        self.nzc = nz * CORES
        self.yb, self.zb = self.nzc * SLOTS, ny * SLOTS
        self.dpn = lax.axis_size("dp")
        self.x = lax.axis_index("dp")
        self.rank = lax.axis_index("expert")
        self.y, self.zc = lax.div(self.rank, self.nzc), lax.rem(self.rank, self.nzc)
        self.c = lax.rem(self.rank, CORES)
        self.z = lax.div(self.zc, CORES)
        self.right = (lax.rem(self.x + 1, self.dpn), self.rank)
        self.left = (lax.rem(self.x + self.dpn - 1, self.dpn), self.rank)
        self.first = self.y * (1 - self.c) + self.z * self.c
        self.second = self.z * (1 - self.c) + self.y * self.c
        self.sibling = (self.x, self.rank + 1 - 2 * self.c)
        self.y_peers = [lax.rem(self.y + k, ny) for k in near_first(ny)]
        self.z_peers = [lax.rem(self.zc + k, self.nzc) for k in near_first(self.nzc)]

    def at_y(self, peer):
        return (self.x, peer * self.nzc + self.zc)

    def at_z(self, peer):
        return (self.x, self.y * self.nzc + peer)

    def at_grid(self, first, second):
        c = self.c
        y_at = first * (1 - c) + second * c
        z_at = second * (1 - c) + first * c
        return (self.x, y_at * self.nzc + z_at * CORES + c)

    def at_near(self, b, core):
        return (lax.rem(self.x + AWAY[b], self.dpn), self.y * self.nzc + self.z * CORES + core)

    def y_block(self, index):
        return pl.ds(pl.multiple_of(index * self.yb, self.yb), self.yb)

    def z_block(self, index):
        return pl.ds(pl.multiple_of(index * self.zb, self.zb), self.zb)


def fore_kernel(ny, nz, spread, scale, *refs):
    src, u, w_in_far, w_out_far, perm, perm_small, perm_x, out, slope, hid, side = refs[:11]
    n = len(spread)
    bufs = [refs[11 + 6 * t : 17 + 6 * t] for t in range(n)]
    at = 11 + 6 * n
    w_in, w_out, acc, hc, hp, po, sib_out, sib_in, st, got, sums, st_b, got_b = refs[at : at + 13]
    near, block, st_c, got_c, half_block, held = refs[at + 13 : at + 19]
    s_y, r_y, s_z, r_z, s_x, r_x, s_o, r_o, s_d, r_d, s_f, r_f, s_g, r_g = refs[at + 19 : at + 33]
    s_b, r_b, s_c, r_c, load = refs[at + 33 :]
    p = Place(ny, nz)
    rows = acc.shape[1]
    half = rows // 2
    top, low = pl.ds(0, half), pl.ds(half, half)
    yb, zb = p.yb, p.zb
    half_width = po.shape[2]
    model_width = 2 * half_width

    pltpu.make_async_copy(w_in_far, w_in, load.at[0]).start()
    pltpu.make_async_copy(w_out_far, w_out, load.at[1]).start()
    others = [p.at_near(b, core) for b in range(1, 4) for core in range(CORES)]
    greet([p.at_y(peer) for peer in p.y_peers] + [p.at_z(peer) for peer in p.z_peers] + others)

    for t, (start, width) in enumerate(spread):
        for peer in p.y_peers:
            send(
                src.at[p.y_block(peer), pl.ds(start, width)],
                bufs[t][0].at[p.y_block(p.y)],
                s_y.at[t],
                r_y.at[t],
                p.at_y(peer),
            )

    own_near = p.x * CORES + p.c
    near_count = 4 * CORES
    for peer in others + [p.sibling]:
        send(u, near.at[own_near], s_g.at[0], r_g.at[0], peer)
    near[own_near] = u[...]

    def stage_z(t):
        ybuf, zsend, zbuf = bufs[t][:3]
        start, width = spread[t]
        ybuf[p.y_block(p.y), :] = src[p.y_block(p.y), start : start + width]
        drain(ybuf.at[pl.ds(0, rows - yb)], r_y.at[t])
        zsend[...] = move_rows(perm[0], ybuf[...])
        for peer in p.z_peers:
            send(zsend.at[p.z_block(peer)], zbuf.at[p.z_block(p.zc)], s_z.at[t], r_z.at[t], p.at_z(peer))
        zbuf[p.z_block(p.zc), :] = zsend[p.z_block(p.zc), :]

    def stage_x(t):
        zbuf, xl, xr = bufs[t][2:5]
        drain(zbuf.at[pl.ds(0, rows - zb)], r_z.at[t])
        send(zbuf, xl, s_x.at[t, 0], r_x.at[t, 0], p.right)
        send(zbuf, xr, s_x.at[t, 1], r_x.at[t, 1], p.left)

    def stage_forward(t):
        xl, xr, xo = bufs[t][3:6]
        drain(xl, r_x.at[t, 0])
        send(xl.at[top], xo.at[top], s_o.at[t, 0], r_o.at[t, 0], p.right)
        drain(xr, r_x.at[t, 1])
        send(xr.at[low], xo.at[low], s_o.at[t, 1], r_o.at[t, 1], p.left)

    def stage_in(t, b):
        start, width = spread[t]
        depth = min(start + width, model_width) - start
        values = bufs[t][2 + b]
        part = jnp.dot(values[:, :depth], w_in[start : start + depth, :], preferred_element_type=jnp.float32)
        acc[b] = part if t == 0 else acc[b] + part
        if t == n - 1:
            side[b] = values[:, depth:]

    def await_far(t):
        xo = bufs[t][5]
        drain(xo.at[top], r_o.at[t, 0])
        drain(xo.at[low], r_o.at[t, 1])

    for t in range(n + 2):
        if t < n:
            stage_z(t)
        if 0 <= t - 1 < n:
            stage_x(t - 1)
        if 0 <= t - 2 < n:
            stage_forward(t - 2)
        if t == 2:
            pltpu.make_async_copy(w_in_far, w_in, load.at[0]).wait()
        if 0 <= t - 3 < n - 1:
            await_far(t - 3)
            for b in range(4):
                stage_in(t - 3, b)

    def hidden_step(b, i, rows_at):
        values = activation(acc[b, rows_at, :])
        hid[b, rows_at, :] = values.astype(jnp.bfloat16)
        gates = side[b, rows_at, :].astype(jnp.float32)
        image = values * (gates[:, 0:1] + gates[:, 1:2])
        text = values * (gates[:, 2:3] + gates[:, 3:4])
        both = jnp.concatenate([image[:ny] + image[ny:], text[:ny] + text[ny:]], 0)
        hc[b, rows_at, :] = both.astype(jnp.bfloat16)

    def half_cols(core):
        return pl.ds(pl.multiple_of(core * half_width, half_width), half_width)

    other = 1 - p.c
    line = [lax.rem(p.first + k, ny) for k in near_first(ny)]

    def stage_line(b):
        drain(sib_in.at[b], r_d.at[b])
        st[b] = (po[b] + sib_in[b].astype(jnp.float32)).astype(jnp.bfloat16)
        for peer in line:
            send(
                st.at[b, p.y_block(peer)], got.at[b, p.first], s_f.at[b], r_f.at[b], p.at_grid(peer, p.second)
            )
        got[b, p.first] = st[b, p.y_block(p.first), :]

    pltpu.make_async_copy(w_out_far, w_out, load.at[1]).wait()
    for b in range(4):
        if b == 3:
            await_far(n - 1)
        stage_in(n - 1, b)
        by_slab(rows, zb, [b], hidden_step)
        hp[0] = move_rows(perm[1 + other], hc[b])
        sib_out[b] = jnp.dot(hp[0], w_out[:, half_cols(other)], preferred_element_type=jnp.float32).astype(
            jnp.bfloat16
        )
        send(sib_out.at[b], sib_in.at[b], s_d.at[b], r_d.at[b], p.sibling)
        hp[1] = move_rows(perm[1 + p.c], hc[b])
        po[b] = jnp.dot(hp[1], w_out[:, half_cols(p.c)], preferred_element_type=jnp.float32)
        if b > 0:
            stage_line(b - 1)
    stage_line(3)

    def slope_step(b, i, rows_at):
        slope[b, rows_at, :] = activation_slope(acc[b, rows_at, :])

    by_slab(rows, zb, range(2), slope_step)

    for b in range(4):
        drain(got.at[b, pl.ds(0, ny - 1)], r_f.at[b])
        total = got[b, 0].astype(jnp.float32)
        for k in range(1, ny):
            total = total + got[b, k].astype(jnp.float32)
        sums[b * yb : (b + 1) * yb, :] = total.astype(jnp.bfloat16)
    st_b[...] = move_rows(perm_small[...], sums[...])
    cut = 4 * CORES * 2

    def cut_block(index):
        return pl.ds(pl.multiple_of(index * cut, cut), cut)

    for k in near_first(ny):
        peer = lax.rem(p.second + k, ny)
        send(st_b.at[cut_block(peer)], got_b.at[p.second], s_g.at[1], r_g.at[1], p.at_grid(p.first, peer))
    got_b[p.second] = st_b[cut_block(p.second), :]
    drain(got_b.at[pl.ds(0, ny - 1)], r_g.at[1])
    total = got_b[0].astype(jnp.float32)
    for k in range(1, ny):
        total = total + got_b[k].astype(jnp.float32)
    part_rows = CORES * 2
    for b in range(4):
        st_c[lax.rem(p.x + AWAY[b], 4)] = total[b * part_rows : (b + 1) * part_rows]
    for b in range(1, 4):
        send(st_c, got_c.at[p.x], s_g.at[2], r_g.at[2], p.at_near(b, p.c))
    got_c[p.x] = st_c[...]
    drain(near.at[pl.ds(0, near_count - 1)], r_g.at[0])
    for k in range(near_count):
        for m in range(2):
            block[m * near_count + k : m * near_count + k + 1, :] = near[k, m : m + 1, :]
    drain(got_c.at[pl.ds(0, 3)], r_g.at[2])
    total = got_c[0] + got_c[1] + got_c[2] + got_c[3]
    for k in range(near_count):
        for m in range(2):
            row = m * near_count + k
            half_sum = jnp.where(p.c == 0, block[row : row + 1, :half_width], block[row : row + 1, half_width:])
            block[row : row + 1, :half_width] = half_sum + total[k // CORES, k % CORES * 2 + m][None]
    half_block[...] = (block[:, :half_width] * scale).astype(jnp.bfloat16)

    c, side_len, second = p.c, ny, p.second
    held[c, second, p.first] = half_block[...]
    for peer in line:
        send(half_block, held.at[c, second, p.first], s_g.at[3], r_g.at[3], p.at_grid(peer, second))
    drain(held.at[c, second, pl.ds(0, side_len - 1)], r_g.at[3])

    def share(slab, k):
        send(slab, slab, s_c.at[k], r_c.at[k], p.sibling)

    share(held.at[c, second], 0)
    right = p.at_grid(p.first, lax.rem(second + 1, side_len))
    left = p.at_grid(p.first, lax.rem(second + side_len - 1, side_len))
    full = side_len // 2 - 1
    for i in range(full):
        r_slab = held.at[c, lax.rem(second + side_len - i, side_len)]
        l_slab = held.at[c, lax.rem(second + i, side_len)]
        send(r_slab, r_slab, s_b.at[i, 0], r_b.at[i, 0], right)
        send(l_slab, l_slab, s_b.at[i, 1], r_b.at[i, 1], left)
        if i == 0:
            by_slab(rows, zb, range(2, 4), slope_step)
        for way, here in enumerate((second + side_len - i - 1, second + i + 1)):
            slab = held.at[c, lax.rem(here, side_len)]
            drain(slab, r_b.at[i, way])
            share(slab, 1 + 2 * i + way)
    parts = (pl.ds(0, side_len // 2), pl.ds(side_len // 2, side_len // 2))
    r_slab = held.at[c, lax.rem(second + side_len - full, side_len), parts[0]]
    l_slab = held.at[c, lax.rem(second + full, side_len), parts[1]]
    send(r_slab, r_slab, s_b.at[full, 0], r_b.at[full, 0], right)
    send(l_slab, l_slab, s_b.at[full, 1], r_b.at[full, 1], left)
    if full == 0:
        by_slab(rows, zb, range(2, 4), slope_step)
    for way in range(2):
        slab = held.at[c, lax.rem(second + side_len // 2, side_len), parts[way]]
        drain(slab, r_b.at[full, way])
        share(slab, 1 + 2 * full + way)
    for k in range(1 + 2 * full):
        drain(held.at[0, 0], r_c.at[k])
    for way in range(2):
        drain(held.at[0, 0, parts[way]], r_c.at[1 + 2 * full + way])
    span = CORES * side_len
    for h in range(CORES):
        for z_at in range(side_len):
            slab = held[h, z_at] if h == 0 else held[h, :, z_at]
            moved = move_rows(perm_x[p.x], slab.reshape(side_len * 2 * near_count, half_width))
            for k in range(2 * 4):
                out[k // 4, k % 4, z_at * span : (z_at + 1) * span, h * half_width : (h + 1) * half_width] = moved[
                    k * span : (k + 1) * span
                ]

    for t in range(n):
        ybuf, zsend, zbuf, xl, xr, xo = bufs[t]
        drain(ybuf.at[pl.ds(0, rows - yb)], s_y.at[t])
        drain(zsend.at[pl.ds(0, rows - zb)], s_z.at[t])
        for way in range(2):
            drain(zbuf, s_x.at[t, way])
            drain(xo.at[top], s_o.at[t, way])
    for b in range(4):
        drain(sib_out.at[b], s_d.at[b])
        drain(got.at[b, pl.ds(0, ny - 1)], s_f.at[b])
    drain(near.at[pl.ds(0, near_count - 1)], s_g.at[0])
    drain(got_b.at[pl.ds(0, ny - 1)], s_g.at[1])
    drain(got_c.at[pl.ds(0, 3)], s_g.at[2])
    drain(held.at[0, 0, pl.ds(0, ny - 1)], s_g.at[3])
    for way in range(2):
        for i in range(full):
            drain(held.at[0, 0], s_b.at[i, way])
        drain(held.at[0, 0, parts[way]], s_b.at[full, way])
        drain(held.at[0, 0, parts[way]], s_c.at[1 + 2 * full + way])
    for k in range(1 + 2 * full):
        drain(held.at[0, 0], s_c.at[k])


def fore_call(experts, seq_len, packed, u, w_in, w_out):
    ny, nz = chip_sides(experts)
    rows = packed.shape[0]
    model_width, hidden = w_in.shape
    half_width = model_width // 2
    spread = spans(model_width, WIDTHS_IN)
    n = len(spread)
    yb, zb, cut = nz * CORES * SLOTS, ny * SLOTS, 4 * CORES * 2
    bf16, f32 = jnp.bfloat16, jnp.float32
    vmem = pl.BlockSpec(memory_space=pltpu.VMEM)
    far = pl.BlockSpec(memory_space=pl.ANY)
    dma = pltpu.SemaphoreType.DMA
    perm = jnp.stack(
        [
            selector((nz * CORES, SLOTS, ny), lambda zc, s, ys: ys * yb + zc * SLOTS + s),
            selector((ny, nz, CORES, 2), lambda ys, zs, cs, m: (zs * CORES + cs) * zb + m * ny + ys),
            selector((nz, ny, CORES, 2), lambda zs, ys, cs, m: (zs * CORES + cs) * zb + m * ny + ys),
        ]
    )
    perm_small = selector((ny, 4, CORES, 2), lambda second, b, cs, m: b * yb + second * 4 + cs * 2 + m)
    perm_x = jnp.stack(
        [
            selector(
                (2, 4, CORES, ny),
                lambda m, b, cs, ys: ys * cut + m * 4 * CORES + (x + np.array(AWAY)[b]) % 4 * CORES + cs,
            )
            for x in range(4)
        ]
    )
    scratch = [pltpu.VMEM((rows, width), bf16) for _, width in spread for _ in range(6)]
    scratch += [
        pltpu.VMEM(w_in.shape, bf16),
        pltpu.VMEM(w_out.shape, bf16),
        pltpu.VMEM((4, rows, hidden), f32),
        pltpu.VMEM((4, rows, hidden), bf16),
        pltpu.VMEM((2, rows, hidden), bf16),
        pltpu.VMEM((4, rows, half_width), f32),
        pltpu.VMEM((4, rows, half_width), bf16),
        pltpu.VMEM((4, rows, half_width), bf16),
        pltpu.VMEM((4, rows, half_width), bf16),
        pltpu.VMEM((4, ny, yb, half_width), bf16),
        pltpu.VMEM((4 * yb, half_width), bf16),
        pltpu.VMEM((4 * yb, half_width), bf16),
        pltpu.VMEM((ny, cut, half_width), bf16),
        pltpu.VMEM((4 * CORES, 2, model_width), f32),
        pltpu.VMEM((cut, model_width), f32),
        pltpu.VMEM((4, CORES * 2, half_width), f32),
        pltpu.VMEM((4, 4, CORES * 2, half_width), f32),
        pltpu.VMEM((cut, half_width), bf16),
        pltpu.VMEM((CORES, nz, ny, cut, half_width), bf16),
    ]
    steps = ny // 2
    scratch += [dma((n,)) for _ in range(4)] + [dma((n, 2)) for _ in range(4)]
    scratch += [dma((4,)) for _ in range(6)]
    scratch += [dma((steps, 2)) for _ in range(2)] + [dma((2 * steps + 1,)) for _ in range(2)] + [dma((2,))]
    return pl.pallas_call(
        functools.partial(fore_kernel, ny, nz, spread, 1.0 / seq_len),
        out_shape=[
            jax.ShapeDtypeStruct((2, 4, experts, model_width), bf16),
            jax.ShapeDtypeStruct((4, rows, hidden), f32),
            jax.ShapeDtypeStruct((4, rows, hidden), bf16),
            jax.ShapeDtypeStruct((4, rows, SIDE), bf16),
        ],
        in_specs=[vmem, vmem, far, far, vmem, vmem, vmem],
        out_specs=[vmem] * 4,
        scratch_shapes=scratch,
        name="moe_fore",
        compiler_params=pltpu.CompilerParams(
            collective_id=0, has_side_effects=True, vmem_limit_bytes=46 * 1024 * 1024
        ),
    )(packed, u, w_in, w_out, perm, perm_small, perm_x)


def back_kernel(ny, nz, spread, *refs):
    d_all, w_in_far, w_out, slope_far, hid_far, side, perm, out = refs[:8]
    n = len(spread)
    bufs = [refs[8 + 12 * t : 20 + 12 * t] for t in range(n)]
    at = 8 + 12 * n
    pulled, d_pre, d_gate, w_in, slope, hid = refs[at : at + 6]
    s_p, r_p, s_q, r_q, s_z, r_z, s_y, r_y, load = refs[at + 6 :]
    loads = [
        pltpu.make_async_copy(w_in_far, w_in, load.at[0]),
        pltpu.make_async_copy(slope_far, slope, load.at[1]),
        pltpu.make_async_copy(hid_far, hid, load.at[2]),
    ]
    for copy in (loads[1], loads[2], loads[0]):
        copy.start()
    p = Place(ny, nz)
    rows = slope_far.shape[1]
    half = rows // 2
    top, low = pl.ds(0, half), pl.ds(half, half)
    yb, zb = p.yb, p.zb
    model_width = w_in_far.shape[0]
    pairs = d_all.shape[1]

    greet(
        [p.at_y(peer) for peer in p.y_peers] + [p.at_z(peer) for peer in p.z_peers] + [p.right, p.left]
    )

    def pull(b):
        part = pl.ds(b * (pairs // 4), pairs // 4)
        for m in range(2):
            pulled[m, part, :] = lax.dot_general(
                d_all[m, part, :], w_out[...], (((1,), (1,)), ((), ())), preferred_element_type=jnp.float32
            )

    def pre_step(b, i, rows_at):
        pair_at = pl.ds(pl.multiple_of(b * (pairs // 4) + i * ny, ny), ny)
        gates = side[b, rows_at, :].astype(jnp.float32)
        image = pulled[0, pair_at, :]
        text = pulled[1, pair_at, :]
        d_act = jnp.concatenate([image, image], 0) * (gates[:, 0:1] + gates[:, 1:2])
        d_act = d_act + jnp.concatenate([text, text], 0) * (gates[:, 2:3] + gates[:, 3:4])
        d_pre[b, rows_at, :] = (d_act * slope[b, rows_at, :]).astype(jnp.bfloat16)
        value = jnp.sum(d_act * hid[b, rows_at, :].astype(jnp.float32), 1, keepdims=True)
        high = value.astype(jnp.bfloat16).astype(jnp.float32)
        lane = lax.broadcasted_iota(jnp.int32, (zb, SIDE), 1)
        d_gate[b, rows_at, :] = jnp.where(
            lane == 2 * p.x, high, jnp.where(lane == 2 * p.x + 1, value - high, 0.0)
        )

    def product_out(b, t):
        start, width = spread[t]
        depth = min(start + width, model_width) - start
        part = lax.dot_general(
            d_pre[b], w_in[start : start + depth, :], (((1,), (1,)), ((), ())), preferred_element_type=jnp.float32
        )
        if t == n - 1:
            part = jnp.concatenate([part, d_gate[b]], 1)
        return part

    def stage_far(t):
        so, sr, sl, ol, orr = bufs[t][:5]
        so[...] = product_out(3, t).astype(jnp.bfloat16)
        send(so.at[top], ol, s_p.at[t, 0], r_p.at[t, 0], p.right)
        send(so.at[low], orr, s_p.at[t, 1], r_p.at[t, 1], p.left)

    def stage_near(t):
        so, sr, sl, ol, orr, fl, fr, zs, zr, ys, yr, own = bufs[t]
        part = product_out(2, t)
        sr[half:, :] = part[half:].astype(jnp.bfloat16)
        drain(ol, r_p.at[t, 0])
        sr[:half, :] = (part[:half] + ol[...].astype(jnp.float32)).astype(jnp.bfloat16)
        send(sr, fl, s_q.at[t, 0], r_q.at[t, 0], p.right)
        part = product_out(1, t)
        sl[:half, :] = part[:half].astype(jnp.bfloat16)
        drain(orr, r_p.at[t, 1])
        sl[half:, :] = (part[half:] + orr[...].astype(jnp.float32)).astype(jnp.bfloat16)
        send(sl, fr, s_q.at[t, 1], r_q.at[t, 1], p.left)
        own[...] = product_out(0, t)

    def stage_back_z(t):
        so, sr, sl, ol, orr, fl, fr, zs, zr, ys, yr, own = bufs[t]
        drain(fl, r_q.at[t, 0])
        drain(fr, r_q.at[t, 1])
        zs[...] = (own[...] + fl[...].astype(jnp.float32) + fr[...].astype(jnp.float32)).astype(jnp.bfloat16)
        for peer in p.z_peers:
            send(zs.at[p.z_block(peer)], zr.at[p.z_block(p.zc)], s_z.at[t], r_z.at[t], p.at_z(peer))
        zr[p.z_block(p.zc), :] = zs[p.z_block(p.zc), :]

    def stage_back_y(t):
        zr, ys, yr = bufs[t][8:11]
        drain(zr.at[pl.ds(0, rows - zb)], r_z.at[t])
        ys[...] = move_rows(perm[...], zr[...])
        for peer in p.y_peers:
            send(ys.at[p.y_block(peer)], yr.at[p.y_block(p.y)], s_y.at[t], r_y.at[t], p.at_y(peer))
        yr[p.y_block(p.y), :] = ys[p.y_block(p.y), :]

    def stage_store(t):
        yr = bufs[t][10]
        start, width = spread[t]
        drain(yr.at[pl.ds(0, rows - yb)], r_y.at[t])
        out[:, start : start + width] = yr[...]

    pull(3)
    loads[1].wait()
    loads[2].wait()
    by_slab(rows, zb, [3], pre_step)
    loads[0].wait()
    for t in range(n):
        stage_far(t)
    for b in range(3):
        pull(b)
    by_slab(rows, zb, range(3), pre_step)
    for t in range(n + 3):
        if t < n:
            stage_near(t)
        if 0 <= t - 1 < n:
            stage_back_z(t - 1)
        if 0 <= t - 2 < n:
            stage_back_y(t - 2)
        if 0 <= t - 3 < n:
            stage_store(t - 3)

    for t in range(n):
        so, sr, sl, ol, orr, fl, fr, zs, zr, ys, yr, own = bufs[t]
        drain(zs.at[pl.ds(0, rows - zb)], s_z.at[t])
        drain(ys.at[pl.ds(0, rows - yb)], s_y.at[t])
        for way in range(2):
            drain(so.at[top], s_p.at[t, way])
            drain(sr, s_q.at[t, way])


def back_call(experts, d_all, w_in, w_out, slope, hid, side):
    ny, nz = chip_sides(experts)
    rows = slope.shape[1]
    model_width, hidden = w_in.shape
    spread = spans(model_width, WIDTHS_OUT)
    n = len(spread)
    half = rows // 2
    bf16, f32 = jnp.bfloat16, jnp.float32
    vmem = pl.BlockSpec(memory_space=pltpu.VMEM)
    dma = pltpu.SemaphoreType.DMA
    scratch = []
    for _, width in spread:
        scratch += [pltpu.VMEM((rows, width), bf16) for _ in range(3)]
        scratch += [pltpu.VMEM((half, width), bf16) for _ in range(2)]
        scratch += [pltpu.VMEM((rows, width), bf16) for _ in range(6)]
        scratch += [pltpu.VMEM((rows, width), f32)]
    scratch += [
        pltpu.VMEM((2, d_all.shape[1], hidden), f32),
        pltpu.VMEM((4, rows, hidden), bf16),
        pltpu.VMEM((4, rows, SIDE), f32),
        pltpu.VMEM(w_in.shape, bf16),
        pltpu.VMEM(slope.shape, f32),
        pltpu.VMEM(hid.shape, bf16),
    ]
    scratch += [dma((n, 2)) for _ in range(4)] + [dma((n,)) for _ in range(4)] + [dma((3,))]
    yb, zb = nz * CORES * SLOTS, ny * SLOTS
    perm = selector((ny, nz * CORES, SLOTS), lambda ys, zc, s: zc * zb + s * ny + ys)
    far = pl.BlockSpec(memory_space=pl.ANY)
    return pl.pallas_call(
        functools.partial(back_kernel, ny, nz, spread),
        out_shape=jax.ShapeDtypeStruct((rows, model_width + SIDE), bf16),
        in_specs=[vmem, far, vmem, far, far, vmem, vmem],
        out_specs=vmem,
        scratch_shapes=scratch,
        name="moe_back",
        compiler_params=pltpu.CompilerParams(
            collective_id=1, has_side_effects=True, vmem_limit_bytes=40 * 1024 * 1024
        ),
    )(d_all, w_in, w_out, slope, hid, side, perm)


def local(tokens, ln_gain, w_router, w_in, w_out, expert_ids, keep, slots, logit_scale):
    pairs_dev, row_width, model_width = tokens.shape
    seq_len = row_width // 2
    token_count = pairs_dev * row_width
    experts = w_router.shape[1]
    capacity = SLOTS
    score_scale = logit_scale[0]
    rows_in = tokens.reshape(token_count, model_width).astype(jnp.float32)
    normed, norm_pull = jax.vjp(lambda values: layer_norm(values, ln_gain), rows_in)
    normed_b = normed.astype(jnp.bfloat16)
    routed = expert_ids.reshape(token_count)
    keep_flat = keep.reshape(token_count)
    target = routed * capacity + slots.reshape(token_count)
    slot_iota = lax.broadcasted_iota(jnp.int32, (experts * capacity, token_count), 0)
    slot_table = ((slot_iota == target[None, :]) & (keep_flat[None, :] == 1)).astype(jnp.bfloat16)
    choose = (lax.broadcasted_iota(jnp.int32, (token_count, experts), 1) == routed[:, None]).astype(
        jnp.float32
    )
    logits = jnp.dot(normed_b, w_router, preferred_element_type=jnp.float32)
    expo = jnp.exp(logits)
    probs = expo / jnp.sum(expo, 1, keepdims=True)
    gate_val = jnp.sum(probs * choose, 1, keepdims=True)
    high = gate_val.astype(jnp.bfloat16).astype(jnp.float32)
    lane = lax.broadcasted_iota(jnp.int32, (token_count, SIDE), 1)
    modality = lax.broadcasted_iota(jnp.int32, (token_count, SIDE), 0) // seq_len
    gate_side = jnp.where(
        lane == 2 * modality, high, jnp.where(lane == 2 * modality + 1, gate_val - high, 0.0)
    ).astype(jnp.bfloat16)
    packed = jnp.dot(
        slot_table, jnp.concatenate([normed_b, gate_side], 1), preferred_element_type=jnp.float32
    ).astype(jnp.bfloat16)
    which = lax.broadcasted_iota(jnp.int32, (2, token_count), 1) // seq_len
    members = (which == lax.broadcasted_iota(jnp.int32, (2, token_count), 0)).astype(jnp.bfloat16)
    token_sums = jnp.dot(
        members, tokens.reshape(token_count, model_width), preferred_element_type=jnp.float32
    )
    everyone, slope, hid, side = fore_call(experts, seq_len, packed, token_sums, w_in[0], w_out[0])
    everyone = everyone.reshape(2, -1, model_width)
    pair_count = everyone.shape[1]
    all_f = everyone.astype(jnp.float32)
    inverse = lax.rsqrt(jnp.sum(all_f * all_f, -1) + norm_eps)
    ny, nz = chip_sides(experts)
    rank = lax.axis_index("expert")
    own_index = (rank % (nz * CORES)) * ny + rank // (nz * CORES)
    scores = (
        jnp.einsum("id,jd->ij", everyone[0], everyone[1], preferred_element_type=jnp.float32)
        * (score_scale * inverse[0])[:, None]
        * inverse[1][None, :]
    )
    row_tot = jax.nn.logsumexp(scores, 1)
    col_tot = jax.nn.logsumexp(scores, 0)
    row_iota = lax.broadcasted_iota(jnp.int32, (pair_count, pair_count), 0)
    eye = (row_iota == lax.broadcasted_iota(jnp.int32, (pair_count, pair_count), 1)).astype(jnp.float32)
    diag_score = jnp.sum(scores * eye, 1)
    losses = (row_tot + col_tot - 2.0 * diag_score) * 0.5
    pair_loss = lax.dynamic_slice_in_dim(losses, own_index, pairs_dev)
    weights = (jnp.exp(scores - row_tot[:, None]) + jnp.exp(scores - col_tot[None, :])) * 0.5 - eye
    d_images = jnp.dot(
        (weights * inverse[1][None, :]).astype(jnp.bfloat16), everyone[1], preferred_element_type=jnp.float32
    )
    d_texts = lax.dot_general(
        (weights * inverse[0][:, None]).astype(jnp.bfloat16),
        everyone[0],
        (((0,), (0,)), ((), ())),
        preferred_element_type=jnp.float32,
    )
    d_units = jnp.stack([d_images, d_texts])
    units = all_f * inverse[:, :, None]
    along = jnp.sum(d_units * units, -1, keepdims=True)
    d_pooled = (d_units - units * along) * (inverse * (score_scale / seq_len))[:, :, None]
    d_own = lax.dynamic_slice_in_dim(d_pooled, own_index, pairs_dev, 1)
    d_mixed = jnp.broadcast_to(d_own, (2, seq_len, model_width)).reshape(token_count, model_width)
    d_back = back_call(experts, d_pooled.astype(jnp.bfloat16), w_in[0], w_out[0], slope, hid, side)
    d_slots = jnp.einsum("st,sd->td", slot_table, d_back, preferred_element_type=jnp.float32)
    d_gate = jnp.sum(d_slots[:, model_width : model_width + 8], 1)
    d_logit = d_gate[:, None] * (choose - probs)
    router_part = jnp.dot(d_logit, w_router.astype(jnp.float32).T, precision=lax.Precision.HIGHEST)
    d_normed = d_slots[:, :model_width] + router_part
    d_tokens = d_mixed + norm_pull(d_normed)[0]
    tokens_grad = (d_tokens * (128.0 * seq_len / score_scale)).astype(jnp.bfloat16)
    return (pair_loss, tokens_grad.reshape(pairs_dev, row_width, model_width))


def solution(mesh):
    in_specs = (
        P(("dp", "expert"), None, None),
        P(),
        P(),
        P("expert", None, "dp"),
        P("expert", "dp", None),
        P(("dp", "expert"), None),
        P(("dp", "expert"), None),
        P(("dp", "expert"), None),
        P(),
    )
    out_specs = (P(("dp", "expert")), P(("dp", "expert"), None, None))
    return jax.shard_map(local, mesh=mesh, in_specs=in_specs, out_specs=out_specs, check_vma=False)
```

```python
import functools
import math

import jax
import jax.numpy as jnp
import numpy as np
from jax import lax
from jax.experimental import pallas as pl
from jax.experimental.pallas import tpu as pltpu
from jax.sharding import PartitionSpec as P

MESH = pl.DeviceIdType.MESH
norm_eps = 1e-06
WIDTHS_IN = (384, 512, 512)
WIDTHS_OUT = (512, 512, 384)
SIDE = 128
AWAY = (0, 3, 1, 2)
CORES = 2
SLOTS = 2


def activation(values):
    return 0.5 * values * (1.0 + lax.erf(values * (0.5**0.5)))


def activation_slope(values):
    bell = jnp.exp(-0.5 * values * values) * 0.3989422804014327
    return 0.5 * (1.0 + lax.erf(values * (0.5**0.5))) + values * bell


def layer_norm(matrix_rows, ln_gain):
    centered = matrix_rows - jnp.mean(matrix_rows, -1, keepdims=True)
    variance = jnp.mean(centered * centered, -1, keepdims=True)
    return centered * lax.rsqrt(variance + norm_eps) * ln_gain.astype(jnp.float32)


def chip_sides(experts):
    chips = experts // CORES
    side = 1
    while side * side < chips:
        side *= 2
    return side, chips // side


def near_first(count):
    offsets = []
    for step in range(1, count // 2 + 1):
        offsets.append(step)
        if count - step != step:
            offsets.append(count - step)
    return offsets


def send(src, dst, send_sem, recv_sem, device):
    pltpu.make_async_remote_copy(
        src_ref=src,
        dst_ref=dst,
        send_sem=send_sem,
        recv_sem=recv_sem,
        device_id=device,
        device_id_type=MESH,
    ).start()


def drain(ref, sem):
    pltpu.make_async_copy(ref, ref, sem).wait()


def greet(peers):
    barrier = pltpu.get_barrier_semaphore()
    for peer in peers:
        pl.semaphore_signal(barrier, inc=1, device_id=peer, device_id_type=MESH)
    pl.semaphore_wait(barrier, len(peers))


def from_slots(slot_table, matrix_rows):
    return jnp.einsum("st,sd->td", slot_table, matrix_rows, preferred_element_type=jnp.float32)


def selector(sizes, source):
    count = math.prod(sizes)
    place = np.arange(count)
    digits = np.unravel_index(place, sizes)
    table = np.zeros((count, count), np.float32)
    table[place, source(*digits)] = 1.0
    return jnp.asarray(table, jnp.bfloat16)


def move_rows(table, values):
    return jnp.dot(table, values, preferred_element_type=jnp.float32).astype(jnp.bfloat16)


def spans(model_width, widths):
    if sum(widths) != model_width + SIDE:
        widths = (model_width // 2, model_width - model_width // 2 + SIDE)
    return [(sum(widths[:t]), widths[t]) for t in range(len(widths))]


def by_slab(rows, slab, blocks, step):
    def body(i, carry):
        for b in blocks:
            step(b, i, pl.ds(pl.multiple_of(i * slab, slab), slab))
        return carry

    lax.fori_loop(0, rows // slab, body, 0)


class Place:
    def __init__(self, ny, nz):
        self.ny, self.nz = ny, nz
        self.nzc = nz * CORES
        self.yb, self.zb = self.nzc * SLOTS, ny * SLOTS
        self.dpn = lax.axis_size("dp")
        self.x = lax.axis_index("dp")
        self.rank = lax.axis_index("expert")
        self.y, self.zc = lax.div(self.rank, self.nzc), lax.rem(self.rank, self.nzc)
        self.c = lax.rem(self.rank, CORES)
        self.z = lax.div(self.zc, CORES)
        self.right = (lax.rem(self.x + 1, self.dpn), self.rank)
        self.left = (lax.rem(self.x + self.dpn - 1, self.dpn), self.rank)
        self.first = self.y * (1 - self.c) + self.z * self.c
        self.second = self.z * (1 - self.c) + self.y * self.c
        self.sibling = (self.x, self.rank + 1 - 2 * self.c)
        self.y_peers = [lax.rem(self.y + k, ny) for k in near_first(ny)]
        self.z_peers = [lax.rem(self.zc + k, self.nzc) for k in near_first(self.nzc)]

    def at_y(self, peer):
        return (self.x, peer * self.nzc + self.zc)

    def at_z(self, peer):
        return (self.x, self.y * self.nzc + peer)

    def at_grid(self, first, second):
        c = self.c
        y_at = first * (1 - c) + second * c
        z_at = second * (1 - c) + first * c
        return (self.x, y_at * self.nzc + z_at * CORES + c)

    def at_near(self, b, core):
        return (lax.rem(self.x + AWAY[b], self.dpn), self.y * self.nzc + self.z * CORES + core)

    def y_block(self, index):
        return pl.ds(pl.multiple_of(index * self.yb, self.yb), self.yb)

    def z_block(self, index):
        return pl.ds(pl.multiple_of(index * self.zb, self.zb), self.zb)


def fore_kernel(ny, nz, spread, scale, *refs):
    src, u, w_in_far, w_out_far, perm, perm_small, perm_x, out, slope, hid, side = refs[:11]
    n = len(spread)
    bufs = [refs[11 + 6 * t : 17 + 6 * t] for t in range(n)]
    at = 11 + 6 * n
    w_in, w_out, acc, hc, hp, po, sib_out, sib_in, st, got, sums, st_b, got_b = refs[at : at + 13]
    near, block, st_c, got_c, half_block, held = refs[at + 13 : at + 19]
    s_y, r_y, s_z, r_z, s_x, r_x, s_o, r_o, s_d, r_d, s_f, r_f, s_g, r_g = refs[at + 19 : at + 33]
    s_b, r_b, s_c, r_c, load = refs[at + 33 :]
    p = Place(ny, nz)
    rows = acc.shape[1]
    half = rows // 2
    top, low = pl.ds(0, half), pl.ds(half, half)
    yb, zb = p.yb, p.zb
    half_width = po.shape[2]
    model_width = 2 * half_width

    pltpu.make_async_copy(w_in_far, w_in, load.at[0]).start()
    pltpu.make_async_copy(w_out_far, w_out, load.at[1]).start()
    others = [p.at_near(b, core) for b in range(1, 4) for core in range(CORES)]
    greet([p.at_y(peer) for peer in p.y_peers] + [p.at_z(peer) for peer in p.z_peers] + others)

    for t, (start, width) in enumerate(spread):
        for peer in p.y_peers:
            send(
                src.at[p.y_block(peer), pl.ds(start, width)],
                bufs[t][0].at[p.y_block(p.y)],
                s_y.at[t],
                r_y.at[t],
                p.at_y(peer),
            )

    own_near = p.x * CORES + p.c
    near_count = 4 * CORES
    for peer in others + [p.sibling]:
        send(u, near.at[own_near], s_g.at[0], r_g.at[0], peer)
    near[own_near] = u[...]

    def stage_z(t):
        ybuf, zsend, zbuf = bufs[t][:3]
        start, width = spread[t]
        ybuf[p.y_block(p.y), :] = src[p.y_block(p.y), start : start + width]
        drain(ybuf.at[pl.ds(0, rows - yb)], r_y.at[t])
        zsend[...] = move_rows(perm[0], ybuf[...])
        for peer in p.z_peers:
            send(zsend.at[p.z_block(peer)], zbuf.at[p.z_block(p.zc)], s_z.at[t], r_z.at[t], p.at_z(peer))
        zbuf[p.z_block(p.zc), :] = zsend[p.z_block(p.zc), :]

    def stage_x(t):
        zbuf, xl, xr = bufs[t][2:5]
        drain(zbuf.at[pl.ds(0, rows - zb)], r_z.at[t])
        send(zbuf, xl, s_x.at[t, 0], r_x.at[t, 0], p.right)
        send(zbuf, xr, s_x.at[t, 1], r_x.at[t, 1], p.left)

    def stage_forward(t):
        xl, xr, xo = bufs[t][3:6]
        drain(xl, r_x.at[t, 0])
        send(xl.at[top], xo.at[top], s_o.at[t, 0], r_o.at[t, 0], p.right)
        drain(xr, r_x.at[t, 1])
        send(xr.at[low], xo.at[low], s_o.at[t, 1], r_o.at[t, 1], p.left)

    def stage_in(t, b):
        start, width = spread[t]
        depth = min(start + width, model_width) - start
        values = bufs[t][2 + b]
        part = jnp.dot(values[:, :depth], w_in[start : start + depth, :], preferred_element_type=jnp.float32)
        acc[b] = part if t == 0 else acc[b] + part
        if t == n - 1:
            side[b] = values[:, depth:]

    def await_far(t):
        xo = bufs[t][5]
        drain(xo.at[top], r_o.at[t, 0])
        drain(xo.at[low], r_o.at[t, 1])

    for t in range(n + 2):
        if t < n:
            stage_z(t)
        if 0 <= t - 1 < n:
            stage_x(t - 1)
        if 0 <= t - 2 < n:
            stage_forward(t - 2)
        if t == 2:
            pltpu.make_async_copy(w_in_far, w_in, load.at[0]).wait()
        if 0 <= t - 3 < n - 1:
            await_far(t - 3)
            for b in range(4):
                stage_in(t - 3, b)

    def hidden_step(b, i, rows_at):
        values = activation(acc[b, rows_at, :])
        hid[b, rows_at, :] = values.astype(jnp.bfloat16)
        gates = side[b, rows_at, :].astype(jnp.float32)
        image = values * (gates[:, 0:1] + gates[:, 1:2])
        text = values * (gates[:, 2:3] + gates[:, 3:4])
        both = jnp.concatenate([image[:ny] + image[ny:], text[:ny] + text[ny:]], 0)
        hc[b, rows_at, :] = both.astype(jnp.bfloat16)

    def half_cols(core):
        return pl.ds(pl.multiple_of(core * half_width, half_width), half_width)

    other = 1 - p.c
    line = [lax.rem(p.first + k, ny) for k in near_first(ny)]

    def stage_line(b):
        drain(sib_in.at[b], r_d.at[b])
        st[b] = (po[b] + sib_in[b].astype(jnp.float32)).astype(jnp.bfloat16)
        for peer in line:
            send(
                st.at[b, p.y_block(peer)], got.at[b, p.first], s_f.at[b], r_f.at[b], p.at_grid(peer, p.second)
            )
        got[b, p.first] = st[b, p.y_block(p.first), :]

    pltpu.make_async_copy(w_out_far, w_out, load.at[1]).wait()
    for b in range(4):
        if b == 3:
            await_far(n - 1)
        stage_in(n - 1, b)
        by_slab(rows, zb, [b], hidden_step)
        hp[0] = move_rows(perm[1 + other], hc[b])
        sib_out[b] = jnp.dot(hp[0], w_out[:, half_cols(other)], preferred_element_type=jnp.float32).astype(
            jnp.bfloat16
        )
        send(sib_out.at[b], sib_in.at[b], s_d.at[b], r_d.at[b], p.sibling)
        hp[1] = move_rows(perm[1 + p.c], hc[b])
        po[b] = jnp.dot(hp[1], w_out[:, half_cols(p.c)], preferred_element_type=jnp.float32)
        if b > 0:
            stage_line(b - 1)
    stage_line(3)

    def slope_step(b, i, rows_at):
        slope[b, rows_at, :] = activation_slope(acc[b, rows_at, :])

    by_slab(rows, zb, range(2), slope_step)

    for b in range(4):
        drain(got.at[b, pl.ds(0, ny - 1)], r_f.at[b])
        total = got[b, 0].astype(jnp.float32)
        for k in range(1, ny):
            total = total + got[b, k].astype(jnp.float32)
        sums[b * yb : (b + 1) * yb, :] = total.astype(jnp.bfloat16)
    st_b[...] = move_rows(perm_small[...], sums[...])
    cut = 4 * CORES * 2

    def cut_block(index):
        return pl.ds(pl.multiple_of(index * cut, cut), cut)

    for k in near_first(ny):
        peer = lax.rem(p.second + k, ny)
        send(st_b.at[cut_block(peer)], got_b.at[p.second], s_g.at[1], r_g.at[1], p.at_grid(p.first, peer))
    got_b[p.second] = st_b[cut_block(p.second), :]
    drain(got_b.at[pl.ds(0, ny - 1)], r_g.at[1])
    total = got_b[0].astype(jnp.float32)
    for k in range(1, ny):
        total = total + got_b[k].astype(jnp.float32)
    part_rows = CORES * 2
    for b in range(4):
        st_c[lax.rem(p.x + AWAY[b], 4)] = total[b * part_rows : (b + 1) * part_rows]
    for b in range(1, 4):
        send(st_c, got_c.at[p.x], s_g.at[2], r_g.at[2], p.at_near(b, p.c))
    got_c[p.x] = st_c[...]
    drain(near.at[pl.ds(0, near_count - 1)], r_g.at[0])
    for k in range(near_count):
        for m in range(2):
            block[m * near_count + k : m * near_count + k + 1, :] = near[k, m : m + 1, :]
    drain(got_c.at[pl.ds(0, 3)], r_g.at[2])
    total = got_c[0] + got_c[1] + got_c[2] + got_c[3]
    for k in range(near_count):
        for m in range(2):
            row = m * near_count + k
            half_sum = jnp.where(p.c == 0, block[row : row + 1, :half_width], block[row : row + 1, half_width:])
            block[row : row + 1, :half_width] = half_sum + total[k // CORES, k % CORES * 2 + m][None]
    half_block[...] = (block[:, :half_width] * scale).astype(jnp.bfloat16)

    c, side_len, second = p.c, ny, p.second
    held[c, second, p.first] = half_block[...]
    for peer in line:
        send(half_block, held.at[c, second, p.first], s_g.at[3], r_g.at[3], p.at_grid(peer, second))
    drain(held.at[c, second, pl.ds(0, side_len - 1)], r_g.at[3])

    def share(slab, k):
        send(slab, slab, s_c.at[k], r_c.at[k], p.sibling)

    share(held.at[c, second], 0)
    right = p.at_grid(p.first, lax.rem(second + 1, side_len))
    left = p.at_grid(p.first, lax.rem(second + side_len - 1, side_len))
    full = side_len // 2 - 1
    for i in range(full):
        r_slab = held.at[c, lax.rem(second + side_len - i, side_len)]
        l_slab = held.at[c, lax.rem(second + i, side_len)]
        send(r_slab, r_slab, s_b.at[i, 0], r_b.at[i, 0], right)
        send(l_slab, l_slab, s_b.at[i, 1], r_b.at[i, 1], left)
        if i == 0:
            by_slab(rows, zb, range(2, 4), slope_step)
        for way, here in enumerate((second + side_len - i - 1, second + i + 1)):
            slab = held.at[c, lax.rem(here, side_len)]
            drain(slab, r_b.at[i, way])
            share(slab, 1 + 2 * i + way)
    parts = (pl.ds(0, side_len // 2), pl.ds(side_len // 2, side_len // 2))
    r_slab = held.at[c, lax.rem(second + side_len - full, side_len), parts[0]]
    l_slab = held.at[c, lax.rem(second + full, side_len), parts[1]]
    send(r_slab, r_slab, s_b.at[full, 0], r_b.at[full, 0], right)
    send(l_slab, l_slab, s_b.at[full, 1], r_b.at[full, 1], left)
    if full == 0:
        by_slab(rows, zb, range(2, 4), slope_step)
    for way in range(2):
        slab = held.at[c, lax.rem(second + side_len // 2, side_len), parts[way]]
        drain(slab, r_b.at[full, way])
        share(slab, 1 + 2 * full + way)
    for k in range(1 + 2 * full):
        drain(held.at[0, 0], r_c.at[k])
    for way in range(2):
        drain(held.at[0, 0, parts[way]], r_c.at[1 + 2 * full + way])
    span = CORES * side_len
    for h in range(CORES):
        for z_at in range(side_len):
            slab = held[h, z_at] if h == 0 else held[h, :, z_at]
            moved = move_rows(perm_x[p.x], slab.reshape(side_len * 2 * near_count, half_width))
            for k in range(2 * 4):
                out[k // 4, k % 4, z_at * span : (z_at + 1) * span, h * half_width : (h + 1) * half_width] = moved[
                    k * span : (k + 1) * span
                ]

    for t in range(n):
        ybuf, zsend, zbuf, xl, xr, xo = bufs[t]
        drain(ybuf.at[pl.ds(0, rows - yb)], s_y.at[t])
        drain(zsend.at[pl.ds(0, rows - zb)], s_z.at[t])
        for way in range(2):
            drain(zbuf, s_x.at[t, way])
            drain(xo.at[top], s_o.at[t, way])
    for b in range(4):
        drain(sib_out.at[b], s_d.at[b])
        drain(got.at[b, pl.ds(0, ny - 1)], s_f.at[b])
    drain(near.at[pl.ds(0, near_count - 1)], s_g.at[0])
    drain(got_b.at[pl.ds(0, ny - 1)], s_g.at[1])
    drain(got_c.at[pl.ds(0, 3)], s_g.at[2])
    drain(held.at[0, 0, pl.ds(0, ny - 1)], s_g.at[3])
    for way in range(2):
        for i in range(full):
            drain(held.at[0, 0], s_b.at[i, way])
        drain(held.at[0, 0, parts[way]], s_b.at[full, way])
        drain(held.at[0, 0, parts[way]], s_c.at[1 + 2 * full + way])
    for k in range(1 + 2 * full):
        drain(held.at[0, 0], s_c.at[k])


def fore_call(experts, seq_len, packed, u, w_in, w_out):
    ny, nz = chip_sides(experts)
    rows = packed.shape[0]
    model_width, hidden = w_in.shape
    half_width = model_width // 2
    spread = spans(model_width, WIDTHS_IN)
    n = len(spread)
    yb, zb, cut = nz * CORES * SLOTS, ny * SLOTS, 4 * CORES * 2
    bf16, f32 = jnp.bfloat16, jnp.float32
    vmem = pl.BlockSpec(memory_space=pltpu.VMEM)
    far = pl.BlockSpec(memory_space=pl.ANY)
    dma = pltpu.SemaphoreType.DMA
    perm = jnp.stack(
        [
            selector((nz * CORES, SLOTS, ny), lambda zc, s, ys: ys * yb + zc * SLOTS + s),
            selector((ny, nz, CORES, 2), lambda ys, zs, cs, m: (zs * CORES + cs) * zb + m * ny + ys),
            selector((nz, ny, CORES, 2), lambda zs, ys, cs, m: (zs * CORES + cs) * zb + m * ny + ys),
        ]
    )
    perm_small = selector((ny, 4, CORES, 2), lambda second, b, cs, m: b * yb + second * 4 + cs * 2 + m)
    perm_x = jnp.stack(
        [
            selector(
                (2, 4, CORES, ny),
                lambda m, b, cs, ys: ys * cut + m * 4 * CORES + (x + np.array(AWAY)[b]) % 4 * CORES + cs,
            )
            for x in range(4)
        ]
    )
    scratch = [pltpu.VMEM((rows, width), bf16) for _, width in spread for _ in range(6)]
    scratch += [
        pltpu.VMEM(w_in.shape, bf16),
        pltpu.VMEM(w_out.shape, bf16),
        pltpu.VMEM((4, rows, hidden), f32),
        pltpu.VMEM((4, rows, hidden), bf16),
        pltpu.VMEM((2, rows, hidden), bf16),
        pltpu.VMEM((4, rows, half_width), f32),
        pltpu.VMEM((4, rows, half_width), bf16),
        pltpu.VMEM((4, rows, half_width), bf16),
        pltpu.VMEM((4, rows, half_width), bf16),
        pltpu.VMEM((4, ny, yb, half_width), bf16),
        pltpu.VMEM((4 * yb, half_width), bf16),
        pltpu.VMEM((4 * yb, half_width), bf16),
        pltpu.VMEM((ny, cut, half_width), bf16),
        pltpu.VMEM((4 * CORES, 2, model_width), f32),
        pltpu.VMEM((cut, model_width), f32),
        pltpu.VMEM((4, CORES * 2, half_width), f32),
        pltpu.VMEM((4, 4, CORES * 2, half_width), f32),
        pltpu.VMEM((cut, half_width), bf16),
        pltpu.VMEM((CORES, nz, ny, cut, half_width), bf16),
    ]
    steps = ny // 2
    scratch += [dma((n,)) for _ in range(4)] + [dma((n, 2)) for _ in range(4)]
    scratch += [dma((4,)) for _ in range(6)]
    scratch += [dma((steps, 2)) for _ in range(2)] + [dma((2 * steps + 1,)) for _ in range(2)] + [dma((2,))]
    return pl.pallas_call(
        functools.partial(fore_kernel, ny, nz, spread, 1.0 / seq_len),
        out_shape=[
            jax.ShapeDtypeStruct((2, 4, experts, model_width), bf16),
            jax.ShapeDtypeStruct((4, rows, hidden), f32),
            jax.ShapeDtypeStruct((4, rows, hidden), bf16),
            jax.ShapeDtypeStruct((4, rows, SIDE), bf16),
        ],
        in_specs=[vmem, vmem, far, far, vmem, vmem, vmem],
        out_specs=[vmem] * 4,
        scratch_shapes=scratch,
        name="moe_fore",
        compiler_params=pltpu.CompilerParams(
            collective_id=0, has_side_effects=True, vmem_limit_bytes=46 * 1024 * 1024
        ),
    )(packed, u, w_in, w_out, perm, perm_small, perm_x)


def back_kernel(ny, nz, spread, *refs):
    d_all, w_in_far, w_out, slope_far, hid_far, side, perm, out = refs[:8]
    n = len(spread)
    bufs = [refs[8 + 12 * t : 20 + 12 * t] for t in range(n)]
    at = 8 + 12 * n
    pulled, d_pre, d_gate, w_in, slope, hid = refs[at : at + 6]
    s_p, r_p, s_q, r_q, s_z, r_z, s_y, r_y, load = refs[at + 6 :]
    loads = [
        pltpu.make_async_copy(w_in_far, w_in, load.at[0]),
        pltpu.make_async_copy(slope_far, slope, load.at[1]),
        pltpu.make_async_copy(hid_far, hid, load.at[2]),
    ]
    for copy in (loads[1], loads[2], loads[0]):
        copy.start()
    p = Place(ny, nz)
    rows = slope_far.shape[1]
    half = rows // 2
    top, low = pl.ds(0, half), pl.ds(half, half)
    yb, zb = p.yb, p.zb
    model_width = w_in_far.shape[0]
    pairs = d_all.shape[1]

    greet(
        [p.at_y(peer) for peer in p.y_peers] + [p.at_z(peer) for peer in p.z_peers] + [p.right, p.left]
    )

    def pull(b):
        part = pl.ds(b * (pairs // 4), pairs // 4)
        for m in range(2):
            pulled[m, part, :] = lax.dot_general(
                d_all[m, part, :], w_out[...], (((1,), (1,)), ((), ())), preferred_element_type=jnp.float32
            )

    def pre_step(b, i, rows_at):
        pair_at = pl.ds(pl.multiple_of(b * (pairs // 4) + i * ny, ny), ny)
        gates = side[b, rows_at, :].astype(jnp.float32)
        image = pulled[0, pair_at, :]
        text = pulled[1, pair_at, :]
        d_act = jnp.concatenate([image, image], 0) * (gates[:, 0:1] + gates[:, 1:2])
        d_act = d_act + jnp.concatenate([text, text], 0) * (gates[:, 2:3] + gates[:, 3:4])
        d_pre[b, rows_at, :] = (d_act * slope[b, rows_at, :]).astype(jnp.bfloat16)
        value = jnp.sum(d_act * hid[b, rows_at, :].astype(jnp.float32), 1, keepdims=True)
        high = value.astype(jnp.bfloat16).astype(jnp.float32)
        lane = lax.broadcasted_iota(jnp.int32, (zb, SIDE), 1)
        d_gate[b, rows_at, :] = jnp.where(
            lane == 2 * p.x, high, jnp.where(lane == 2 * p.x + 1, value - high, 0.0)
        )

    def product_out(b, t):
        start, width = spread[t]
        depth = min(start + width, model_width) - start
        part = lax.dot_general(
            d_pre[b], w_in[start : start + depth, :], (((1,), (1,)), ((), ())), preferred_element_type=jnp.float32
        )
        if t == n - 1:
            part = jnp.concatenate([part, d_gate[b]], 1)
        return part

    def stage_far(t):
        so, sr, sl, ol, orr = bufs[t][:5]
        so[...] = product_out(3, t).astype(jnp.bfloat16)
        send(so.at[top], ol, s_p.at[t, 0], r_p.at[t, 0], p.right)
        send(so.at[low], orr, s_p.at[t, 1], r_p.at[t, 1], p.left)

    def stage_near(t):
        so, sr, sl, ol, orr, fl, fr, zs, zr, ys, yr, own = bufs[t]
        part = product_out(2, t)
        sr[half:, :] = part[half:].astype(jnp.bfloat16)
        drain(ol, r_p.at[t, 0])
        sr[:half, :] = (part[:half] + ol[...].astype(jnp.float32)).astype(jnp.bfloat16)
        send(sr, fl, s_q.at[t, 0], r_q.at[t, 0], p.right)
        part = product_out(1, t)
        sl[:half, :] = part[:half].astype(jnp.bfloat16)
        drain(orr, r_p.at[t, 1])
        sl[half:, :] = (part[half:] + orr[...].astype(jnp.float32)).astype(jnp.bfloat16)
        send(sl, fr, s_q.at[t, 1], r_q.at[t, 1], p.left)
        own[...] = product_out(0, t)

    def stage_back_z(t):
        so, sr, sl, ol, orr, fl, fr, zs, zr, ys, yr, own = bufs[t]
        drain(fl, r_q.at[t, 0])
        drain(fr, r_q.at[t, 1])
        zs[...] = (own[...] + fl[...].astype(jnp.float32) + fr[...].astype(jnp.float32)).astype(jnp.bfloat16)
        for peer in p.z_peers:
            send(zs.at[p.z_block(peer)], zr.at[p.z_block(p.zc)], s_z.at[t], r_z.at[t], p.at_z(peer))
        zr[p.z_block(p.zc), :] = zs[p.z_block(p.zc), :]

    def stage_back_y(t):
        zr, ys, yr = bufs[t][8:11]
        drain(zr.at[pl.ds(0, rows - zb)], r_z.at[t])
        ys[...] = move_rows(perm[...], zr[...])
        for peer in p.y_peers:
            send(ys.at[p.y_block(peer)], yr.at[p.y_block(p.y)], s_y.at[t], r_y.at[t], p.at_y(peer))
        yr[p.y_block(p.y), :] = ys[p.y_block(p.y), :]

    def stage_store(t):
        yr = bufs[t][10]
        start, width = spread[t]
        drain(yr.at[pl.ds(0, rows - yb)], r_y.at[t])
        out[:, start : start + width] = yr[...]

    pull(3)
    loads[1].wait()
    loads[2].wait()
    by_slab(rows, zb, [3], pre_step)
    loads[0].wait()
    for t in range(n):
        stage_far(t)
    for b in range(3):
        pull(b)
    by_slab(rows, zb, range(3), pre_step)
    for t in range(n + 3):
        if t < n:
            stage_near(t)
        if 0 <= t - 1 < n:
            stage_back_z(t - 1)
        if 0 <= t - 2 < n:
            stage_back_y(t - 2)
        if 0 <= t - 3 < n:
            stage_store(t - 3)

    for t in range(n):
        so, sr, sl, ol, orr, fl, fr, zs, zr, ys, yr, own = bufs[t]
        drain(zs.at[pl.ds(0, rows - zb)], s_z.at[t])
        drain(ys.at[pl.ds(0, rows - yb)], s_y.at[t])
        for way in range(2):
            drain(so.at[top], s_p.at[t, way])
            drain(sr, s_q.at[t, way])


def back_call(experts, d_all, w_in, w_out, slope, hid, side):
    ny, nz = chip_sides(experts)
    rows = slope.shape[1]
    model_width, hidden = w_in.shape
    spread = spans(model_width, WIDTHS_OUT)
    n = len(spread)
    half = rows // 2
    bf16, f32 = jnp.bfloat16, jnp.float32
    vmem = pl.BlockSpec(memory_space=pltpu.VMEM)
    dma = pltpu.SemaphoreType.DMA
    scratch = []
    for _, width in spread:
        scratch += [pltpu.VMEM((rows, width), bf16) for _ in range(3)]
        scratch += [pltpu.VMEM((half, width), bf16) for _ in range(2)]
        scratch += [pltpu.VMEM((rows, width), bf16) for _ in range(6)]
        scratch += [pltpu.VMEM((rows, width), f32)]
    scratch += [
        pltpu.VMEM((2, d_all.shape[1], hidden), f32),
        pltpu.VMEM((4, rows, hidden), bf16),
        pltpu.VMEM((4, rows, SIDE), f32),
        pltpu.VMEM(w_in.shape, bf16),
        pltpu.VMEM(slope.shape, f32),
        pltpu.VMEM(hid.shape, bf16),
    ]
    scratch += [dma((n, 2)) for _ in range(4)] + [dma((n,)) for _ in range(4)] + [dma((3,))]
    yb, zb = nz * CORES * SLOTS, ny * SLOTS
    perm = selector((ny, nz * CORES, SLOTS), lambda ys, zc, s: zc * zb + s * ny + ys)
    far = pl.BlockSpec(memory_space=pl.ANY)
    return pl.pallas_call(
        functools.partial(back_kernel, ny, nz, spread),
        out_shape=jax.ShapeDtypeStruct((rows, model_width + SIDE), bf16),
        in_specs=[vmem, far, vmem, far, far, vmem, vmem],
        out_specs=vmem,
        scratch_shapes=scratch,
        name="moe_back",
        compiler_params=pltpu.CompilerParams(
            collective_id=1, has_side_effects=True, vmem_limit_bytes=40 * 1024 * 1024
        ),
    )(d_all, w_in, w_out, slope, hid, side, perm)


def local(tokens, ln_gain, w_router, w_in, w_out, expert_ids, keep, slots, logit_scale):
    pairs_dev, row_width, model_width = tokens.shape
    seq_len = row_width // 2
    token_count = pairs_dev * row_width
    experts = w_router.shape[1]
    capacity = SLOTS
    score_scale = logit_scale[0]
    rows_in = tokens.reshape(token_count, model_width).astype(jnp.float32)
    normed, norm_pull = jax.vjp(lambda values: layer_norm(values, ln_gain), rows_in)
    normed_b = normed.astype(jnp.bfloat16)
    routed = expert_ids.reshape(token_count)
    keep_flat = keep.reshape(token_count)
    target = routed * capacity + slots.reshape(token_count)
    slot_iota = lax.broadcasted_iota(jnp.int32, (experts * capacity, token_count), 0)
    slot_table = ((slot_iota == target[None, :]) & (keep_flat[None, :] == 1)).astype(jnp.bfloat16)
    choose = (lax.broadcasted_iota(jnp.int32, (token_count, experts), 1) == routed[:, None]).astype(
        jnp.float32
    )
    logits = jnp.dot(normed_b, w_router, preferred_element_type=jnp.float32)
    expo = jnp.exp(logits)
    probs = expo / jnp.sum(expo, 1, keepdims=True)
    gate_val = jnp.sum(probs * choose, 1, keepdims=True)
    high = gate_val.astype(jnp.bfloat16).astype(jnp.float32)
    lane = lax.broadcasted_iota(jnp.int32, (token_count, SIDE), 1)
    modality = lax.broadcasted_iota(jnp.int32, (token_count, SIDE), 0) // seq_len
    gate_side = jnp.where(
        lane == 2 * modality, high, jnp.where(lane == 2 * modality + 1, gate_val - high, 0.0)
    ).astype(jnp.bfloat16)
    packed = jnp.dot(
        slot_table, jnp.concatenate([normed_b, gate_side], 1), preferred_element_type=jnp.float32
    ).astype(jnp.bfloat16)
    which = lax.broadcasted_iota(jnp.int32, (2, token_count), 1) // seq_len
    members = (which == lax.broadcasted_iota(jnp.int32, (2, token_count), 0)).astype(jnp.bfloat16)
    token_sums = jnp.dot(
        members, tokens.reshape(token_count, model_width), preferred_element_type=jnp.float32
    )
    everyone, slope, hid, side = fore_call(experts, seq_len, packed, token_sums, w_in[0], w_out[0])
    everyone = everyone.reshape(2, -1, model_width)
    pair_count = everyone.shape[1]
    all_f = everyone.astype(jnp.float32)
    inverse = lax.rsqrt(jnp.sum(all_f * all_f, -1) + norm_eps)
    ny, nz = chip_sides(experts)
    rank = lax.axis_index("expert")
    own_index = (rank % (nz * CORES)) * ny + rank // (nz * CORES)
    scores = (
        jnp.einsum("id,jd->ij", everyone[0], everyone[1], preferred_element_type=jnp.float32)
        * (score_scale * inverse[0])[:, None]
        * inverse[1][None, :]
    )
    row_tot = jax.nn.logsumexp(scores, 1)
    col_tot = jax.nn.logsumexp(scores, 0)
    row_iota = lax.broadcasted_iota(jnp.int32, (pair_count, pair_count), 0)
    eye = (row_iota == lax.broadcasted_iota(jnp.int32, (pair_count, pair_count), 1)).astype(jnp.float32)
    diag_score = jnp.sum(scores * eye, 1)
    losses = (row_tot + col_tot - 2.0 * diag_score) * 0.5
    pair_loss = lax.dynamic_slice_in_dim(losses, own_index, pairs_dev)
    weights = (jnp.exp(scores - row_tot[:, None]) + jnp.exp(scores - col_tot[None, :])) * 0.5 - eye
    d_images = jnp.dot(
        (weights * inverse[1][None, :]).astype(jnp.bfloat16), everyone[1], preferred_element_type=jnp.float32
    )
    d_texts = lax.dot_general(
        (weights * inverse[0][:, None]).astype(jnp.bfloat16),
        everyone[0],
        (((0,), (0,)), ((), ())),
        preferred_element_type=jnp.float32,
    )
    d_units = jnp.stack([d_images, d_texts])
    units = all_f * inverse[:, :, None]
    along = jnp.sum(d_units * units, -1, keepdims=True)
    d_pooled = (d_units - units * along) * (inverse * (score_scale / seq_len))[:, :, None]
    d_own = lax.dynamic_slice_in_dim(d_pooled, own_index, pairs_dev, 1)
    d_mixed = jnp.broadcast_to(d_own, (2, seq_len, model_width)).reshape(token_count, model_width)
    d_back = back_call(experts, d_pooled.astype(jnp.bfloat16), w_in[0], w_out[0], slope, hid, side)
    d_slots = jnp.einsum("st,sd->td", slot_table, d_back, preferred_element_type=jnp.float32)
    d_gate = jnp.sum(d_slots[:, model_width : model_width + 8], 1)
    d_logit = d_gate[:, None] * (choose - probs)
    router_part = jnp.dot(d_logit, w_router.astype(jnp.float32).T, precision=lax.Precision.HIGHEST)
    d_normed = d_slots[:, :model_width] + router_part
    d_tokens = d_mixed + norm_pull(d_normed)[0]
    tokens_grad = (d_tokens * (128.0 * seq_len / score_scale)).astype(jnp.bfloat16)
    return (pair_loss, tokens_grad.reshape(pairs_dev, row_width, model_width))


def solution(mesh):
    in_specs = (
        P(("dp", "expert"), None, None),
        P(),
        P(),
        P("expert", None, "dp"),
        P("expert", "dp", None),
        P(("dp", "expert"), None),
        P(("dp", "expert"), None),
        P(("dp", "expert"), None),
        P(),
    )
    out_specs = (P(("dp", "expert")), P(("dp", "expert"), None, None))
    return jax.shard_map(local, mesh=mesh, in_specs=in_specs, out_specs=out_specs, check_vma=False)
```
